512 devices in a mesh: rep: 8 (over z_lo), sp: 8 (over x, core), tp: 8 (over z_hi, y).
Axes of the slice: x: 4, y: 4, z: 16 (z_hi: 2, z_lo: 8; z = z_hi * 8 + z_lo), core: 2. Of those that a mesh axis runs over, the one named last changes fastest.
Arguments:
- latents: bfloat16 [8, 1, 1536, 5120], P('rep', None, 'sp'), may hold values from -6 to 6
- timesteps: int32 [8], P('rep'), may hold values from 0 to 49
- mod_table: float32 [50, 2, 5120], replicated, may hold values from -2 to 2
- w_query: bfloat16 [5120, 3072], P('rep', 'tp'), may hold values from -1 to 1
- w_key: bfloat16 [5120, 3072], P('rep', 'tp'), may hold values from -1 to 1
- w_value: bfloat16 [5120, 3072], P('rep', 'tp'), may hold values from -0.078125 to 0.078125
- q_gain: float32 [3072], replicated, may hold values from 0 to 4
- k_gain: float32 [3072], replicated, may hold values from 0 to 4
Outputs:
- context: bfloat16 [8, 1, 1536, 3072], P('rep', None, 'sp', 'tp')
The draws below stay inside these ranges and needn't reach their ends.
All inputs are finite; a program needn't handle non-finite values.
Results may differ from the reference program's by a relative error of at most 0.0057.
Values may be sent and summed in bfloat16 or wider, within the bound.
A program may use at most 64 MiB of HBM per device.

```python
import jax
import jax.numpy as jnp
from jax import lax

D = 5120
HEAD_DIM = 128
HEADS = 24
INNER = 3072
SEQ = 1536
CLIPS = 1
STEPS = 50
GROUPS = 8


def shared_query(key):
    return jax.random.truncated_normal(key, -3.0, 3.0, (D, INNER), jnp.float32) * D ** (-0.5)


def draw_w_query(key, part):
    base = shared_query(key)
    return base.astype(jnp.bfloat16)


def draw_w_key(key, part):
    key = jax.random.fold_in(key, 11)
    fresh = jax.random.truncated_normal(key, -3.0, 3.0, (D, INNER), jnp.float32) * D ** (-0.5)
    mixed = fresh
    return mixed.astype(jnp.bfloat16)


def gain_values(key, spread_log):
    return jnp.exp(jax.random.uniform(key, (INNER,), jnp.float32, jnp.log(0.5), jnp.log(0.5) + spread_log))


def draw_q_gain(key, part):
    key = jax.random.fold_in(key, 21)
    return gain_values(key, 1.6)


def draw_k_gain(key, part):
    key = jax.random.fold_in(key, 22)
    return gain_values(key, 1.6)


def set_ends(array, stream_key, smallest, largest):
    longest = array.shape.index(max(array.shape))
    spots = []
    for shift in (0, 1):
        where = [jax.random.randint(jax.random.fold_in(stream_key, axis), (), 0, length) for axis, length in enumerate(array.shape)]
        where[longest] = (where[longest] + shift) % array.shape[longest]
        spots.append(tuple(where))
    return array.at[spots[0]].set(smallest).at[spots[1]].set(largest)


def block_levels(key, extent, shards, smallest, top_value):
    level = 1.0
    for axis_at, shards_of in shards:
        steps = jax.random.uniform(jax.random.fold_in(jax.random.fold_in(key, 6), axis_at), (shards_of,), jnp.float32, smallest / len(shards), top_value / len(shards))
        level = level * jnp.repeat(jnp.exp(steps), extent[axis_at] // shards_of).reshape((-1,) + (1,) * (len(extent) - 1 - axis_at))
    return level


def gaussian(rng, extent, width, limit, split=(), kind=jnp.bfloat16):
    values = jax.random.normal(rng, extent, jnp.float32) * width
    if len(split) > 0:
        values = block_levels(rng, extent, split, -0.22, 0.18) * values
    return jnp.clip(values, min=-limit, max=limit).astype(kind)


def setup_inputs(seed: int = 0) -> dict:
    splits = jax.random.split(jax.random.key(seed), 9)
    return {
        "latents": gaussian(splits[0], (GROUPS, CLIPS, SEQ, D), 1.0, 6.0, ((0, 8), (2, 8))),
        "timesteps": set_ends(jax.random.randint(splits[1], (GROUPS,), 0, STEPS), jax.random.fold_in(splits[1], 1), 0, STEPS - 1).astype(jnp.int32),
        "mod_table": gaussian(splits[2], (STEPS, 2, D), 0.4, 2.0, (), jnp.float32),
        "w_query": draw_w_query(jax.random.fold_in(splits[8], 71), 0),
        "w_key": draw_w_key(jax.random.fold_in(splits[8], 71), 0),
        "w_value": gaussian(splits[5], (D, INNER), D ** -0.5, 0.078125, ((0, 8), (1, 8))),
        "q_gain": draw_q_gain(jax.random.fold_in(splits[8], 71), 0),
        "k_gain": draw_k_gain(jax.random.fold_in(splits[8], 71), 0),
    }


def clip_attention(query, keys, vals):
    qf = query.astype(jnp.float32).reshape(SEQ, HEADS, HEAD_DIM)
    kf = keys.astype(jnp.float32).reshape(SEQ, HEADS, HEAD_DIM)
    vf = vals.astype(jnp.float32).reshape(SEQ, HEADS, HEAD_DIM)
    scores = jnp.einsum('qhd,khd->hqk', qf, kf, precision=lax.Precision.HIGHEST) / jnp.sqrt(jnp.float32(HEAD_DIM))
    weights = jnp.exp(scores - lax.optimization_barrier(jnp.max(scores, axis=-1, keepdims=True)))
    total = lax.optimization_barrier(jnp.sum(weights, axis=-1))
    rounded = weights.astype(jnp.bfloat16).astype(jnp.float32)
    out = jnp.einsum('hqk,khd->qhd', rounded, vf, precision=lax.Precision.HIGHEST)
    out = out / jnp.swapaxes(total, 0, 1)[..., None]
    return out.reshape(SEQ, INNER).astype(jnp.bfloat16)

def qk_norm(values, gain):
    vf = values.astype(jnp.float32)
    return (vf * gain * lax.rsqrt(lax.optimization_barrier(jnp.mean(vf * vf, axis=-1, keepdims=True)) + 1e-06)).astype(jnp.bfloat16)

def reference(latents, timesteps, mod_table, w_query, w_key, w_value, q_gain, k_gain):

    def one_group(inputs):
        clips_in, step_index = inputs
        onehot = (jnp.arange(STEPS, dtype=jnp.int32) == step_index).astype(jnp.float32)
        modulation = jnp.dot(onehot, mod_table.reshape(STEPS, 2 * D), precision=lax.Precision.HIGHEST).reshape(2, D)
        values = clips_in.astype(jnp.float32)
        center = values - lax.optimization_barrier(jnp.mean(values, axis=-1, keepdims=True))
        spread = lax.optimization_barrier(jnp.mean(center * center, axis=-1, keepdims=True))
        normed = (center * lax.rsqrt(spread + 1e-06) * (1.0 + modulation[1]) + modulation[0]).astype(jnp.bfloat16)
        flat = normed.reshape(CLIPS * SEQ, D)
        query = qk_norm(jnp.dot(flat, w_query, preferred_element_type=jnp.float32).astype(jnp.bfloat16), q_gain)
        keys = qk_norm(jnp.dot(flat, w_key, preferred_element_type=jnp.float32).astype(jnp.bfloat16), k_gain)
        vals = jnp.dot(flat, w_value, preferred_element_type=jnp.float32).astype(jnp.bfloat16)
        triple = (query.reshape(CLIPS, SEQ, INNER), keys.reshape(CLIPS, SEQ, INNER), vals.reshape(CLIPS, SEQ, INNER))
        return lax.map(lambda item: clip_attention(item[0], item[1], item[2]), triple)
    return lax.map(one_group, (latents, timesteps))
```

```python
import jax
import jax.numpy as jnp
from jax import lax
from jax.sharding import PartitionSpec as P

HEAD_DIM = 128


def local(latents, timesteps, mod_table, w_query, w_key, w_value, q_gain, k_gain):
    seq_dev, width = latents.shape[2], latents.shape[3]
    cols = w_query.shape[1]
    heads = cols // HEAD_DIM
    sp = lax.axis_size("sp")
    part = w_query.shape[0] // sp
    stacked = jnp.concatenate(
        [lax.dynamic_slice_in_dim(w, lax.axis_index("sp") * part, part, 0) for w in (w_query, w_key, w_value)],
        axis=1,
    )
    weights = lax.all_gather(stacked, ("rep", "sp"), axis=0, tiled=True)

    modulation = lax.dynamic_index_in_dim(mod_table, timesteps[0], 0, keepdims=False)
    values = latents.reshape(seq_dev, width).astype(jnp.float32)
    center = values - jnp.mean(values, axis=-1, keepdims=True)
    spread = jnp.mean(center * center, axis=-1, keepdims=True)
    normed = (center * lax.rsqrt(spread + 1e-06) * (1.0 + modulation[1]) + modulation[0]).astype(jnp.bfloat16)

    projected = jnp.dot(normed, weights, preferred_element_type=jnp.float32).astype(jnp.bfloat16)
    query, keys, vals = (projected[:, i * cols : (i + 1) * cols] for i in range(3))
    pair = jnp.stack([query, keys]).astype(jnp.float32)
    inner = cols * lax.axis_size("tp")
    square = lax.psum(jnp.sum(pair * pair, axis=-1), "tp") / inner
    start = lax.axis_index("tp") * cols
    gains = jnp.stack([lax.dynamic_slice_in_dim(g, start, cols, 0) for g in (q_gain, k_gain)])
    pair = (pair * gains[:, None, :] * lax.rsqrt(square[..., None] + 1e-06)).astype(jnp.bfloat16)

    both = lax.all_gather(jnp.stack([pair[1], vals]), "sp", axis=1, tiled=True)
    qh = pair[0].reshape(seq_dev, heads, HEAD_DIM)
    kh = both[0].reshape(-1, heads, HEAD_DIM)
    vh = both[1].reshape(-1, heads, HEAD_DIM)
    scores = jnp.einsum("qhd,khd->hqk", qh, kh, preferred_element_type=jnp.float32) / jnp.sqrt(jnp.float32(HEAD_DIM))
    soft = jnp.exp(scores - jnp.max(scores, axis=-1, keepdims=True))
    total = jnp.sum(soft, axis=-1)
    out = jnp.einsum("hqk,khd->qhd", soft.astype(jnp.bfloat16), vh, preferred_element_type=jnp.float32)
    out = (out / jnp.swapaxes(total, 0, 1)[..., None]).astype(jnp.bfloat16)
    return out.reshape(1, 1, seq_dev, cols)


def solution(mesh):
    return jax.shard_map(
        local,
        mesh=mesh,
        in_specs=(
            P("rep", None, "sp", None),
            P("rep"),
            P(),
            P("rep", "tp"),
            P("rep", "tp"),
            P("rep", "tp"),
            P(),
            P(),
        ),
        out_specs=P("rep", None, "sp", "tp"),
        check_vma=False,
    )
```

```python
import functools

import jax
import jax.numpy as jnp
from jax import lax
from jax.experimental import pallas as pl
from jax.experimental.pallas import tpu as pltpu
from jax.sharding import PartitionSpec as P

HEAD_DIM = 128
SKEW = 2
LAG_X = 1
LAG_F = 2
MESH = pl.DeviceIdType.MESH


def dot(a, b, dims=((1,), (0,)), precision=None):
    return lax.dot_general(a, b, (dims, ((), ())), precision=precision, preferred_element_type=jnp.float32)


def kernel(
    sizes,
    steps_ref, latents_hbm, table_hbm, wk_hbm, wv_hbm, wq_hbm, kgain_ref, qgain_ref,
    out_ref,
    wbuf, latents, table, modulation, normed, acc, kvbuf, qbuf, sums,
    local_sem, zrecv, zrest, xrecv, srecv, kvrecv, kvsib, sumrecv, zsend, xsend, ssend, sumsend,
):
    nz, nx, nt = sizes
    r, s, tp = lax.axis_index("rep"), lax.axis_index("sp"), lax.axis_index("tp")
    x, c = s // 2, s % 2
    step = 1 - 2 * c
    fore, back = (x + step + nx) % nx, (x - step + nx) % nx
    base = c * nx
    mine, of_back, of_fore, of_far = base + x, base + back, base + fore, base + (x + 2) % nx
    to_fore, to_back, to_core = {"sp": fore * 2 + c}, {"sp": back * 2 + c}, {"sp": s + 1 - 2 * c}
    up, down = {"rep": r + 1}, {"rep": r - 1}
    whbm = (wk_hbm, wv_hbm, wq_hbm)
    rows, width = latents.shape
    cols = kvbuf.shape[3]
    heads = cols // HEAD_DIM

    def send(src, dst, send_sem, recv_sem, where):
        pltpu.make_async_remote_copy(src, dst, send_sem, recv_sem, device_id=where, device_id_type=MESH).start()

    def arrived(ref, recv_sem):
        pltpu.make_async_remote_copy(ref, ref, xsend.at[0], recv_sem, device_id=to_fore, device_id_type=MESH).wait_recv()

    def sent(ref, send_sem):
        pltpu.make_async_remote_copy(ref, ref, send_sem, sumrecv.at[0], device_id=to_fore, device_id_type=MESH).wait_send()

    loads = [pltpu.make_async_copy(latents_hbm, latents, local_sem.at[0]),
             pltpu.make_async_copy(table_hbm, table, local_sem.at[1])]
    loads += [pltpu.make_async_copy(whbm[m], wbuf.at[m, r], local_sem.at[2 + m]) for m in range(3)]
    for load in loads:
        load.start()

    barrier = pltpu.get_barrier_semaphore()

    def greet(where):
        pl.semaphore_signal(barrier, inc=1, device_id=where, device_id_type=MESH)

    for where in (to_fore, to_back, to_core):
        greet(where)
    for i in range(1, nt):
        greet({"tp": (tp + i) % nt})
    pl.when(r < nz - 1)(lambda: greet(up))
    pl.when(r > 0)(lambda: greet(down))
    inside = jnp.logical_and(r > 0, r < nz - 1)
    pl.when(inside)(lambda: pl.semaphore_wait(barrier, 4 + nt))
    pl.when(jnp.logical_not(inside))(lambda: pl.semaphore_wait(barrier, 3 + nt))

    def both_ways(action):
        pl.when(r < nz - 1)(lambda: action(up, 0))
        pl.when(r > 0)(lambda: action(down, 1))

    def send_own(m):
        both_ways(lambda where, way: send(whbm[m].at[mine], wbuf.at[m, r, mine], zsend.at[m], zrecv.at[m, r], where))

    def send_rest(m):
        def one(where, way):
            for i in range(1, nx):
                piece = base + (x + i) % nx
                send(whbm[m].at[piece], wbuf.at[m, r, piece], zsend.at[m], zrest.at[m, way], where)
        both_ways(one)

    def over_sources(k, least, action):
        pl.when(jnp.logical_and(k >= least, r - k >= 0))(lambda: action(r - k, 0))
        pl.when(jnp.logical_and(k >= least, r + k <= nz - 1))(lambda: action(r + k, 1))

    def z_event(k, m):
        def one(src, way):
            piece = wbuf.at[m, src, mine]
            arrived(piece, zrecv.at[m, src])
            if way == 0:
                pl.when(r < nz - 1)(lambda: send(piece, piece, zsend.at[m], zrecv.at[m, src], up))
            else:
                pl.when(r > 0)(lambda: send(piece, piece, zsend.at[m], zrecv.at[m, src], down))

            @pl.when(k >= 2)
            def _():
                send(piece, piece, xsend.at[m], xrecv.at[0, m, src], to_fore)
                send(piece, piece, xsend.at[m], xrecv.at[1, m, src], to_back)
        over_sources(k, 1, one)

    def x_event(k, m):
        def one(src, way):
            piece = wbuf.at[m, src, of_back]
            arrived(piece, xrecv.at[0, m, src])
            send(piece, piece, xsend.at[m], xrecv.at[2, m, src], to_fore)
        over_sources(k, 2, one)

    def to_sibling(m, src):
        block = wbuf.at[m, src, pl.ds(base, nx)]
        send(block, block, ssend.at[m], srecv.at[m], to_core)

    def f_event(k, m):
        def one(src, way):
            arrived(wbuf.at[m, src, of_fore], xrecv.at[1, m, src])
            arrived(wbuf.at[m, src, of_far], xrecv.at[2, m, src])
            to_sibling(m, src)
        over_sources(k, 2, one)

    def rest_event(m):
        def one(src, way):
            arrived(wbuf.at[m, src, pl.ds(0, nx - 1)], zrest.at[m, way])
            to_sibling(m, src)
        over_sources(1, 1, one)

    def slot(t):
        for m in range(3):
            z_event(t - SKEW * m, m)
        for m in range(3):
            x_event(t - SKEW * m - LAG_X, m)
        for m in range(3):
            f_event(t - SKEW * m - LAG_F, m)

    def slots(first, end, extra=None):
        @pl.loop(first, end)
        def _(t):
            slot(t)
            if extra is not None:
                extra(t - first)

    norm_rows = rows // 6 if rows % 96 == 0 else rows // 2

    def norm_block(i):
        at = pl.ds(pl.multiple_of(i * norm_rows, norm_rows), norm_rows)
        values = latents[at, :].astype(jnp.float32)
        center = values - jnp.mean(values, axis=-1, keepdims=True)
        spread = jnp.mean(center * center, axis=-1, keepdims=True)
        scaled = center * lax.rsqrt(spread + 1e-06) * modulation[1:2, :] + modulation[0:1, :]
        normed[at, :] = scaled.astype(jnp.bfloat16)

    def project(m):
        arrived(wbuf.at[m, pl.ds(0, nz - 1), pl.ds(0, nx)], srecv.at[m])
        depth = width // nz
        acc[...] = jnp.zeros_like(acc)

        @pl.loop(0, nz)
        def _(src):
            at = pl.ds(pl.multiple_of(src * depth, HEAD_DIM), depth)
            acc[...] += dot(normed[:, at], wbuf[m, src].reshape(depth, cols))
        return acc[...].astype(jnp.bfloat16)

    def send_sums(i, values):
        wide = values.astype(jnp.float32)
        square = dot(jnp.ones((8, cols), jnp.float32), wide * wide, ((1,), (1,)), lax.Precision.HIGHEST)
        sums[i, tp] = jnp.zeros(sums.shape[2:], jnp.float32)
        sums[i, tp, :, 0:rows] = square[0:1]
        for j in range(1, nt):
            send(sums.at[i, tp], sums.at[i, tp], sumsend.at[i], sumrecv.at[i], {"tp": (tp + j) % nt})

    def normalise(i, values, gain_ref):
        arrived(sums.at[i, pl.ds(0, nt - 1)], sumrecv.at[i])
        total = sums[i, 0]
        for j in range(1, nt):
            total = total + sums[i, j]
        scale = lax.rsqrt(total * (1.0 / (nt * cols)) + 1e-06)
        column = jnp.concatenate(
            [jnp.transpose(jnp.broadcast_to(scale[:, j : j + 128], (128, 128))) for j in range(0, scale.shape[1], 128)],
            axis=0,
        )[0:rows]
        gain = gain_ref[:, pl.ds(pl.multiple_of(tp * cols, HEAD_DIM), cols)]
        wide = values.astype(jnp.float32) * gain
        parts = [wide[:, h * 128 : (h + 1) * 128] * column for h in range(heads)]
        return jnp.concatenate(parts, axis=1).astype(jnp.bfloat16)

    def kv_send(j):
        block = kvbuf.at[j, mine]
        send(block, block, xsend.at[3 + j], kvrecv.at[0, j], to_fore)
        send(block, block, xsend.at[3 + j], kvrecv.at[1, j], to_back)
        send(block, block, ssend.at[3 + j], kvsib.at[j], to_core)

    def kv_pass(j):
        block = kvbuf.at[j, of_back]
        arrived(block, kvrecv.at[0, j])
        send(block, block, xsend.at[3 + j], kvrecv.at[2, j], to_fore)
        send(block, block, ssend.at[3 + j], kvsib.at[j], to_core)

    def kv_far(j):
        for kind, piece in ((1, of_fore), (2, of_far)):
            block = kvbuf.at[j, piece]
            arrived(block, kvrecv.at[kind, j])
            send(block, block, ssend.at[3 + j], kvsib.at[j], to_core)

    send_own(0)
    send_rest(0)
    send_own(1)
    loads[1].wait()
    modulation[...] = table[steps_ref[0]]
    modulation[1:2, :] = modulation[1:2, :] + 1.0
    loads[0].wait()

    def early(i):
        norm_block(i)
        pl.when(i == 0)(lambda: send_own(2))
        pl.when(i == 1)(lambda: send_rest(1))
        pl.when(i == 3)(lambda: send_rest(2))

    slots(1, 1 + rows // norm_rows, early)
    for load in loads[2:]:
        load.wait()
    ends = [nz - 1 + SKEW * m + LAG_F for m in range(3)]
    done = 1 + rows // norm_rows
    rest_event(0)
    slots(done, ends[0] + 1)
    keys = project(0)
    send_sums(0, keys)
    kvbuf[0, mine] = keys
    rest_event(1)
    slots(ends[0] + 1, ends[1])
    kvbuf[0, mine] = normalise(0, kvbuf[0, mine], kgain_ref)
    kv_send(0)
    rest_event(2)
    slots(ends[1], ends[1] + 1)
    kvbuf[1, mine] = project(1)
    kv_send(1)
    kv_pass(0)
    slots(ends[1] + 1, ends[2] + 1)
    kv_far(0)
    kv_pass(1)
    kv_far(1)
    query = project(2)
    send_sums(1, query)
    arrived(kvbuf.at[0, pl.ds(0, nx)], kvsib.at[0])
    arrived(kvbuf.at[1, pl.ds(0, nx)], kvsib.at[1])
    qbuf[...] = normalise(1, query, qgain_ref)

    inverse_root = 1.0 / HEAD_DIM**0.5
    for h in range(heads):
        at = slice(h * HEAD_DIM, (h + 1) * HEAD_DIM)
        kh = kvbuf[0, :, :, at].reshape(2 * nx * rows, HEAD_DIM)
        vh = kvbuf[1, :, :, at].reshape(2 * nx * rows, HEAD_DIM)
        scores = dot(qbuf[:, at], kh, ((1,), (1,))) * inverse_root
        weights = jnp.exp(scores - jnp.max(scores, axis=-1, keepdims=True))
        total = jnp.sum(weights, axis=-1, keepdims=True)
        out_ref[:, at] = (dot(weights.astype(jnp.bfloat16), vh) / total).astype(jnp.bfloat16)


    def pieces(m, count):
        outer = max(a for a in range(1, nz + 1) if count % a == 0 and count // a <= 2 * nx)
        return wbuf.at[m, pl.ds(0, outer), pl.ds(0, count // outer)]

    def wait_sends(z_count, x_count):
        for m in range(3):
            sent(pieces(m, z_count), zsend.at[m])
            sent(pieces(m, x_count), xsend.at[m])

    pl.when(inside)(lambda: wait_sends(2 * nx + nz - 1, 3 * (nz - 3)))
    pl.when(jnp.logical_not(inside))(lambda: wait_sends(nx, 3 * (nz - 2)))
    for m in range(3):
        sent(wbuf.at[m, pl.ds(0, nz - 1), pl.ds(0, nx)], ssend.at[m])
    for j in range(2):
        sent(kvbuf.at[j, pl.ds(0, 3)], xsend.at[3 + j])
        sent(kvbuf.at[j, pl.ds(0, nx)], ssend.at[3 + j])
        sent(sums.at[j, pl.ds(0, nt - 1)], sumsend.at[j])


def local(sizes, latents, timesteps, mod_table, w_query, w_key, w_value, q_gain, k_gain):
    nz, nx, nt = sizes
    rows, width = latents.shape[2:]
    cols = w_query.shape[1]
    part = w_query.shape[0] // (2 * nx)
    hbm, vmem = pl.BlockSpec(memory_space=pl.ANY), pl.BlockSpec(memory_space=pltpu.VMEM)
    split = [w.reshape(2 * nx, part, cols) for w in (w_key, w_value, w_query)]
    dma = pltpu.SemaphoreType.DMA
    out = pl.pallas_call(
        functools.partial(kernel, sizes),
        out_shape=jax.ShapeDtypeStruct((rows, cols), jnp.bfloat16),
        in_specs=[pl.BlockSpec(memory_space=pltpu.SMEM), hbm, hbm, hbm, hbm, hbm, vmem, vmem],
        out_specs=vmem,
        scratch_shapes=[
            pltpu.VMEM((3, nz, 2 * nx, part, cols), jnp.bfloat16),
            pltpu.VMEM((rows, width), jnp.bfloat16),
            pltpu.VMEM(mod_table.shape, jnp.float32),
            pltpu.VMEM((2, width), jnp.float32),
            pltpu.VMEM((rows, width), jnp.bfloat16),
            pltpu.VMEM((rows, cols), jnp.float32),
            pltpu.VMEM((2, 2 * nx, rows, cols), jnp.bfloat16),
            pltpu.VMEM((rows, cols), jnp.bfloat16),
            pltpu.VMEM((2, nt, 1, (rows + 127) // 128 * 128), jnp.float32),
            dma((5,)),
            dma((3, nz)),
            dma((3, 2)),
            dma((3, 3, nz)),
            dma((3,)),
            dma((3, 2)),
            dma((2,)),
            dma((2,)),
            dma((3,)),
            dma((5,)),
            dma((5,)),
            dma((2,)),
        ],
        compiler_params=pltpu.CompilerParams(
            collective_id=0, has_side_effects=True, vmem_limit_bytes=48 * 1024 * 1024
        ),
    )(
        timesteps,
        latents.reshape(rows, width),
        mod_table,
        *split,
        k_gain.reshape(1, -1),
        q_gain.reshape(1, -1),
    )
    return out.reshape(1, 1, rows, cols)


def solution(mesh):
    sizes = (mesh.shape["rep"], mesh.shape["sp"] // 2, mesh.shape["tp"])
    return jax.shard_map(
        functools.partial(local, sizes),
        mesh=mesh,
        in_specs=(
            P("rep", None, "sp", None),
            P("rep"),
            P(),
            P("rep", "tp"),
            P("rep", "tp"),
            P("rep", "tp"),
            P(),
            P(),
        ),
        out_specs=P("rep", None, "sp", "tp"),
        check_vma=False,
    )
```

```python
import functools

import jax
import jax.numpy as jnp
from jax import lax
from jax.experimental import pallas as pl
from jax.experimental.pallas import tpu as pltpu
from jax.sharding import PartitionSpec as P

HEAD_DIM = 128
SKEW = 2
LAG_X = 1
LAG_F = 2
LAG_G = 3
MESH = pl.DeviceIdType.MESH


def dot(a, b, dims=((1,), (0,)), precision=None):
    return lax.dot_general(a, b, (dims, ((), ())), precision=precision, preferred_element_type=jnp.float32)


def kernel(
    sizes,
    steps_ref, latents_hbm, table_hbm, wk_hbm, wq_hbm, wv_hbm, kgain_ref, qgain_ref,
    out_ref,
    wbuf, latents, table, modulation, normed, acc, kvbuf, qbuf, probs, sums, token,
    local_sem, zrecv, zrest, xrecv, srecv, kvrecv, kvsib, sumrecv, zsend, xsend, ssend, sumsend,
):
    nz, nx, nt = sizes
    r, s, tp = lax.axis_index("rep"), lax.axis_index("sp"), lax.axis_index("tp")
    x, c = s // 2, s % 2
    step = 1 - 2 * c
    fore, back = (x + step + nx) % nx, (x - step + nx) % nx
    base = c * nx
    mine, of_back, of_fore, of_far = base + x, base + back, base + fore, base + (x + 2) % nx
    to_fore, to_back, to_core = {"sp": fore * 2 + c}, {"sp": back * 2 + c}, {"sp": s + 1 - 2 * c}
    up, down = {"rep": r + 1}, {"rep": r - 1}
    whbm = (wk_hbm, wq_hbm, wv_hbm)
    rows, width = latents.shape
    cols = kvbuf.shape[3]
    heads = cols // HEAD_DIM

    def send(src, dst, send_sem, recv_sem, where):
        pltpu.make_async_remote_copy(src, dst, send_sem, recv_sem, device_id=where, device_id_type=MESH).start()

    def arrived(ref, recv_sem):
        pltpu.make_async_remote_copy(ref, ref, xsend.at[0], recv_sem, device_id=to_fore, device_id_type=MESH).wait_recv()

    def sent(ref, send_sem):
        pltpu.make_async_remote_copy(ref, ref, send_sem, sumrecv.at[0], device_id=to_fore, device_id_type=MESH).wait_send()

    loads = [pltpu.make_async_copy(latents_hbm, latents, local_sem.at[0]),
             pltpu.make_async_copy(table_hbm, table, local_sem.at[1])]
    loads += [pltpu.make_async_copy(whbm[m], wbuf.at[m, r], local_sem.at[2 + m]) for m in range(3)]
    for load in loads:
        load.start()

    barrier = pltpu.get_barrier_semaphore()

    def greet(where):
        pl.semaphore_signal(barrier, inc=1, device_id=where, device_id_type=MESH)

    ny = nt // 2
    place = (tp // ny) * nz + r

    def on_ring(z):
        z = (z + 2 * nz) % (2 * nz)
        return {"rep": z % nz, "tp": (z // nz) * ny + tp % ny}

    ring_up, ring_down = on_ring(place + 1), on_ring(place - 1)
    for where in (to_fore, to_back, to_core, ring_up, ring_down):
        greet(where)
    for i in range(1, ny):
        greet({"tp": (tp // ny) * ny + (tp + i) % ny})
    pl.semaphore_wait(barrier, 4 + ny)

    def pass_token():
        pl.semaphore_signal(token, inc=1, device_id=ring_up, device_id_type=MESH)

    def token_event(t):
        @pl.when(t <= nz)
        def _():
            pl.semaphore_wait(token, 1)
            pl.when(t < nz)(pass_token)

    pass_token()

    def both_ways(action):
        pl.when(r < nz - 1)(lambda: action(up, 0))
        pl.when(r > 0)(lambda: action(down, 1))

    def send_own(m):
        both_ways(lambda where, way: send(whbm[m].at[mine], wbuf.at[m, r, mine], zsend.at[m], zrecv.at[m, r], where))

    def send_rest(m):
        def one(where, way):
            for i in range(1, nx):
                piece = base + (x + i) % nx
                send(whbm[m].at[piece], wbuf.at[m, r, piece], zsend.at[m], zrest.at[m, way], where)
        both_ways(one)

    def over_sources(k, least, action):
        pl.when(jnp.logical_and(k >= least, r - k >= 0))(lambda: action(r - k, 0))
        pl.when(jnp.logical_and(k >= least, r + k <= nz - 1))(lambda: action(r + k, 1))

    def z_event(k, m):
        def one(src, way):
            piece = wbuf.at[m, src, mine]
            arrived(piece, zrecv.at[m, src])
            if way == 0:
                pl.when(r < nz - 1)(lambda: send(piece, piece, zsend.at[m], zrecv.at[m, src], up))
            else:
                pl.when(r > 0)(lambda: send(piece, piece, zsend.at[m], zrecv.at[m, src], down))

            @pl.when(k >= 2)
            def _():
                send(piece, piece, xsend.at[m], xrecv.at[0, m, src], to_fore)
                send(piece, piece, xsend.at[m], xrecv.at[1, m, src], to_back)
        over_sources(k, 1, one)

    def x_event(k, m):
        def one(src, way):
            piece = wbuf.at[m, src, of_back]
            arrived(piece, xrecv.at[0, m, src])
            send(piece, piece, xsend.at[m], xrecv.at[2, m, src], to_fore)
        over_sources(k, 2, one)

    def to_sibling(m, src):
        block = wbuf.at[m, src, pl.ds(base, nx)]
        send(block, block, ssend.at[m], srecv.at[m, src], to_core)

    def f_event(k, m):
        def one(src, way):
            arrived(wbuf.at[m, src, of_fore], xrecv.at[1, m, src])
            arrived(wbuf.at[m, src, of_far], xrecv.at[2, m, src])
            to_sibling(m, src)
        over_sources(k, 2, one)

    def rest_event(m):
        def one(src, way):
            arrived(wbuf.at[m, src, pl.ds(0, nx - 1)], zrest.at[m, way])
            to_sibling(m, src)
        over_sources(1, 1, one)

    def add_source(m, src):
        depth = width // nz
        at = pl.ds(pl.multiple_of(src * depth, HEAD_DIM), depth)
        acc[m] += dot(normed[:, at], wbuf[m, src].reshape(depth, cols))

    def use(m, src):
        arrived(wbuf.at[m, src, pl.ds(base, nx)], srecv.at[m, src])
        add_source(m, src)

    def g_event(k, least):
        over_sources(k, least, lambda src, way: use(2, src))

    def slot(t):
        for m in range(3):
            z_event(t - SKEW * m, m)
        for m in range(3):
            x_event(t - SKEW * m - LAG_X, m)
        for m in range(3):
            f_event(t - SKEW * m - LAG_F, m)
        g_event(t - SKEW * 2 - LAG_G, 2)
        token_event(t)

    def slots(first, end, extra=None):
        @pl.loop(first, end)
        def _(t):
            slot(t)
            if extra is not None:
                extra(t - first)

    norm_rows = rows // 6 if rows % 96 == 0 else rows // 2

    def norm_block(i):
        at = pl.ds(pl.multiple_of(i * norm_rows, norm_rows), norm_rows)
        values = latents[at, :].astype(jnp.float32)
        center = values - jnp.mean(values, axis=-1, keepdims=True)
        spread = jnp.mean(center * center, axis=-1, keepdims=True)
        scaled = center * lax.rsqrt(spread + 1e-06) * modulation[1:2, :] + modulation[0:1, :]
        normed[at, :] = scaled.astype(jnp.bfloat16)

    def project(m):
        @pl.loop(0, nz)
        def _(src):
            pl.when(src == r)(lambda: add_source(m, src))
            pl.when(src != r)(lambda: use(m, src))

    def send_sums(i, values):
        wide = values.astype(jnp.float32)
        square = dot(jnp.ones((8, cols), jnp.float32), wide * wide, ((1,), (1,)), lax.Precision.HIGHEST)
        sums[i, tp] = jnp.zeros(sums.shape[2:], jnp.float32)
        sums[i, tp, :, 0:rows] = square[0:1]
        for j in range(1, nt):
            send(sums.at[i, tp], sums.at[i, tp], sumsend.at[i], sumrecv.at[i], {"tp": (tp + j) % nt})

    def normalise(i, values, gain_ref):
        arrived(sums.at[i, pl.ds(0, nt - 1)], sumrecv.at[i])
        total = sums[i, 0]
        for j in range(1, nt):
            total = total + sums[i, j]
        scale = lax.rsqrt(total * (1.0 / (nt * cols)) + 1e-06)
        column = jnp.concatenate(
            [jnp.transpose(jnp.broadcast_to(scale[:, j : j + 128], (128, 128))) for j in range(0, scale.shape[1], 128)],
            axis=0,
        )[0:rows]
        gain = gain_ref[:, pl.ds(pl.multiple_of(tp * cols, HEAD_DIM), cols)]
        wide = values.astype(jnp.float32) * gain
        parts = [wide[:, h * 128 : (h + 1) * 128] * column for h in range(heads)]
        return jnp.concatenate(parts, axis=1).astype(jnp.bfloat16)

    def kv_send(j):
        block = kvbuf.at[j, mine]
        send(block, block, xsend.at[3 + j], kvrecv.at[0, j], to_fore)
        send(block, block, xsend.at[3 + j], kvrecv.at[1, j], to_back)
        send(block, block, ssend.at[3 + j], kvsib.at[j], to_core)

    def kv_pass(j):
        block = kvbuf.at[j, of_back]
        arrived(block, kvrecv.at[0, j])
        send(block, block, xsend.at[3 + j], kvrecv.at[2, j], to_fore)
        send(block, block, ssend.at[3 + j], kvsib.at[j], to_core)

    def kv_far(j):
        for kind, piece in ((1, of_fore), (2, of_far)):
            block = kvbuf.at[j, piece]
            arrived(block, kvrecv.at[kind, j])
            send(block, block, ssend.at[3 + j], kvsib.at[j], to_core)

    send_own(0)
    send_rest(0)
    send_own(1)
    acc[...] = jnp.zeros_like(acc)
    loads[1].wait()
    modulation[...] = table[steps_ref[0]]
    modulation[1:2, :] = modulation[1:2, :] + 1.0
    loads[0].wait()

    def early(i):
        norm_block(i)
        pl.when(i == 0)(lambda: send_own(2))
        pl.when(i == 1)(lambda: send_rest(1))
        pl.when(i == 3)(lambda: send_rest(2))

    done = 1 + rows // norm_rows
    slots(1, done, early)
    for load in loads[2:]:
        load.wait()
    add_source(2, r)
    ends = [nz + SKEW * m + LAG_F for m in range(2)]
    last = nz + SKEW * 2 + LAG_G
    rest_event(0)
    slots(done, ends[0])
    project(0)
    kvbuf[0, mine] = acc[0].astype(jnp.bfloat16)
    send_sums(0, kvbuf[0, mine])
    rest_event(1)
    slots(ends[0], ends[1])
    project(1)
    qbuf[...] = acc[1].astype(jnp.bfloat16)
    send_sums(1, qbuf[...])
    rest_event(2)
    slots(ends[1], last - 1)
    g_event(1, 1)
    kvbuf[0, mine] = normalise(0, kvbuf[0, mine], kgain_ref)
    kv_send(0)
    slots(last - 1, last)
    kvbuf[1, mine] = acc[2].astype(jnp.bfloat16)
    kv_send(1)
    kv_pass(0)
    qbuf[...] = normalise(1, qbuf[...], qgain_ref)
    kv_far(0)
    kv_pass(1)
    arrived(kvbuf.at[0, pl.ds(0, nx)], kvsib.at[0])

    inverse_root = 1.0 / HEAD_DIM**0.5
    keys_all = 2 * nx * rows
    totals = []
    for h in range(heads):
        at = slice(h * HEAD_DIM, (h + 1) * HEAD_DIM)
        scores = dot(qbuf[:, at], kvbuf[0, :, :, at].reshape(keys_all, HEAD_DIM), ((1,), (1,))) * inverse_root
        weights = jnp.exp(scores - jnp.max(scores, axis=-1, keepdims=True))
        totals.append(jnp.sum(weights, axis=-1, keepdims=True))
        probs[h] = weights.astype(jnp.bfloat16)
        if h == 0:
            kv_far(1)
    arrived(kvbuf.at[1, pl.ds(0, nx)], kvsib.at[1])
    for h in range(heads):
        at = slice(h * HEAD_DIM, (h + 1) * HEAD_DIM)
        context = dot(probs[h], kvbuf[1, :, :, at].reshape(keys_all, HEAD_DIM)) / totals[h]
        out_ref[:, at] = context.astype(jnp.bfloat16)

    inside = jnp.logical_and(r > 0, r < nz - 1)

    def pieces(m, count):
        outer = max(a for a in range(1, nz + 1) if count % a == 0 and count // a <= 2 * nx)
        return wbuf.at[m, pl.ds(0, outer), pl.ds(0, count // outer)]

    def wait_sends(z_count, x_count):
        for m in range(3):
            sent(pieces(m, z_count), zsend.at[m])
            sent(pieces(m, x_count), xsend.at[m])

    pl.when(inside)(lambda: wait_sends(2 * nx + nz - 1, 3 * (nz - 3)))
    pl.when(jnp.logical_not(inside))(lambda: wait_sends(nx, 3 * (nz - 2)))
    for m in range(3):
        sent(wbuf.at[m, pl.ds(0, nz - 1), pl.ds(0, nx)], ssend.at[m])
    for j in range(2):
        sent(kvbuf.at[j, pl.ds(0, 3)], xsend.at[3 + j])
        sent(kvbuf.at[j, pl.ds(0, nx)], ssend.at[3 + j])
        sent(sums.at[j, pl.ds(0, nt - 1)], sumsend.at[j])


def local(sizes, latents, timesteps, mod_table, w_query, w_key, w_value, q_gain, k_gain):
    nz, nx, nt = sizes
    rows, width = latents.shape[2:]
    cols = w_query.shape[1]
    part = w_query.shape[0] // (2 * nx)
    hbm, vmem = pl.BlockSpec(memory_space=pl.ANY), pl.BlockSpec(memory_space=pltpu.VMEM)
    split = [w.reshape(2 * nx, part, cols) for w in (w_key, w_query, w_value)]
    dma = pltpu.SemaphoreType.DMA
    out = pl.pallas_call(
        functools.partial(kernel, sizes),
        out_shape=jax.ShapeDtypeStruct((rows, cols), jnp.bfloat16),
        in_specs=[pl.BlockSpec(memory_space=pltpu.SMEM), hbm, hbm, hbm, hbm, hbm, vmem, vmem],
        out_specs=vmem,
        scratch_shapes=[
            pltpu.VMEM((3, nz, 2 * nx, part, cols), jnp.bfloat16),
            pltpu.VMEM((rows, width), jnp.bfloat16),
            pltpu.VMEM(mod_table.shape, jnp.float32),
            pltpu.VMEM((2, width), jnp.float32),
            pltpu.VMEM((rows, width), jnp.bfloat16),
            pltpu.VMEM((3, rows, cols), jnp.float32),
            pltpu.VMEM((2, 2 * nx, rows, cols), jnp.bfloat16),
            pltpu.VMEM((rows, cols), jnp.bfloat16),
            pltpu.VMEM((cols // HEAD_DIM, rows, 2 * nx * rows), jnp.bfloat16),
            pltpu.VMEM((2, nt, 1, (rows + 127) // 128 * 128), jnp.float32),
            pltpu.SemaphoreType.REGULAR,
            dma((5,)),
            dma((3, nz)),
            dma((3, 2)),
            dma((3, 3, nz)),
            dma((3, nz)),
            dma((3, 2)),
            dma((2,)),
            dma((2,)),
            dma((3,)),
            dma((5,)),
            dma((5,)),
            dma((2,)),
        ],
        compiler_params=pltpu.CompilerParams(
            collective_id=0, has_side_effects=True, vmem_limit_bytes=62 * 1024 * 1024
        ),
    )(
        timesteps,
        latents.reshape(rows, width),
        mod_table,
        *split,
        k_gain.reshape(1, -1),
        q_gain.reshape(1, -1),
    )
    return out.reshape(1, 1, rows, cols)


def solution(mesh):
    sizes = (mesh.shape["rep"], mesh.shape["sp"] // 2, mesh.shape["tp"])
    return jax.shard_map(
        functools.partial(local, sizes),
        mesh=mesh,
        in_specs=(
            P("rep", None, "sp", None),
            P("rep"),
            P(),
            P("rep", "tp"),
            P("rep", "tp"),
            P("rep", "tp"),
            P(),
            P(),
        ),
        out_specs=P("rep", None, "sp", "tp"),
        check_vma=False,
    )
```

```python
import functools

import jax
import jax.numpy as jnp
from jax import lax
from jax.experimental import pallas as pl
from jax.experimental.pallas import tpu as pltpu
from jax.sharding import PartitionSpec as P

HEAD_DIM = 128
OFFSETS = (0, 1, 3)
REST_1 = 3
REST_2 = 9
LAG_X = 1
LAG_F = 2
LAG_G = 3
MESH = pl.DeviceIdType.MESH


def dot(a, b, dims=((1,), (0,)), precision=None):
    return lax.dot_general(a, b, (dims, ((), ())), precision=precision, preferred_element_type=jnp.float32)


def kernel(
    sizes,
    steps_ref, latents_hbm, table_hbm, wk_hbm, wq_hbm, wv_hbm, kgain_ref, qgain_ref,
    out_ref,
    wbuf, latents, table, modulation, normed, acc, kvbuf, qbuf, probs, sums, scales, scale_row, token,
    local_sem, zrecv, zrest, xrecv, srecv, kvrecv, kvsib, sumrecv, scalerecv, zsend, xsend, ssend, sumsend, scalesend,
):
    nz, nx, nt = sizes
    r, s, tp = lax.axis_index("rep"), lax.axis_index("sp"), lax.axis_index("tp")
    x, c = s // 2, s % 2
    step = 1 - 2 * c
    fore, back = (x + step + nx) % nx, (x - step + nx) % nx
    base = c * nx
    mine, of_back, of_fore, of_far = base + x, base + back, base + fore, base + (x + 2) % nx
    to_fore, to_back, to_core = {"sp": fore * 2 + c}, {"sp": back * 2 + c}, {"sp": s + 1 - 2 * c}
    up, down = {"rep": r + 1}, {"rep": r - 1}
    whbm = (wk_hbm, wq_hbm, wv_hbm)
    rows, width = latents.shape
    cols = kvbuf.shape[3]
    heads = cols // HEAD_DIM

    def send(src, dst, send_sem, recv_sem, where):
        pltpu.make_async_remote_copy(src, dst, send_sem, recv_sem, device_id=where, device_id_type=MESH).start()

    def arrived(ref, recv_sem):
        pltpu.make_async_remote_copy(ref, ref, xsend.at[0], recv_sem, device_id=to_fore, device_id_type=MESH).wait_recv()

    def sent(ref, send_sem):
        pltpu.make_async_remote_copy(ref, ref, send_sem, sumrecv.at[0], device_id=to_fore, device_id_type=MESH).wait_send()

    loads = [pltpu.make_async_copy(latents_hbm, latents, local_sem.at[0]),
             pltpu.make_async_copy(table_hbm, table, local_sem.at[1])]
    loads += [pltpu.make_async_copy(whbm[m], wbuf.at[m, r], local_sem.at[2 + m]) for m in range(3)]
    for load in loads:
        load.start()

    barrier = pltpu.get_barrier_semaphore()

    def greet(where):
        pl.semaphore_signal(barrier, inc=1, device_id=where, device_id_type=MESH)

    ny = nt // 2
    place = (tp // ny) * nz + r

    def on_ring(z):
        z = (z + 2 * nz) % (2 * nz)
        return {"rep": z % nz, "tp": (z // nz) * ny + tp % ny}

    ring_up, ring_down = on_ring(place + 1), on_ring(place - 1)
    for where in (to_fore, to_back, to_core, ring_up, ring_down):
        greet(where)
    for i in range(1, ny):
        greet({"tp": (tp // ny) * ny + (tp + i) % ny})
    pl.semaphore_wait(barrier, 4 + ny)

    def pass_token():
        pl.semaphore_signal(token, inc=1, device_id=ring_up, device_id_type=MESH)

    def token_event(t):
        @pl.when(t <= nz)
        def _():
            pl.semaphore_wait(token, 1)
            pl.when(t < nz)(pass_token)

    pass_token()

    def both_ways(action):
        pl.when(r < nz - 1)(lambda: action(up, 0))
        pl.when(r > 0)(lambda: action(down, 1))

    def send_own(m):
        both_ways(lambda where, way: send(whbm[m].at[mine], wbuf.at[m, r, mine], zsend.at[m], zrecv.at[m, r], where))

    def send_rest(m):
        def one(where, way):
            for i in range(1, nx):
                piece = base + (x + i) % nx
                send(whbm[m].at[piece], wbuf.at[m, r, piece], zsend.at[m], zrest.at[m, way], where)
        both_ways(one)

    def over_sources(k, least, action):
        pl.when(jnp.logical_and(k >= least, r - k >= 0))(lambda: action(r - k, 0))
        pl.when(jnp.logical_and(k >= least, r + k <= nz - 1))(lambda: action(r + k, 1))

    def z_event(k, m):
        def one(src, way):
            piece = wbuf.at[m, src, mine]
            arrived(piece, zrecv.at[m, src])
            if way == 0:
                pl.when(r < nz - 1)(lambda: send(piece, piece, zsend.at[m], zrecv.at[m, src], up))
            else:
                pl.when(r > 0)(lambda: send(piece, piece, zsend.at[m], zrecv.at[m, src], down))

            @pl.when(k >= 2)
            def _():
                send(piece, piece, xsend.at[m], xrecv.at[0, m, src], to_fore)
                send(piece, piece, xsend.at[m], xrecv.at[1, m, src], to_back)
        over_sources(k, 1, one)

    def x_event(k, m):
        def one(src, way):
            piece = wbuf.at[m, src, of_back]
            arrived(piece, xrecv.at[0, m, src])
            send(piece, piece, xsend.at[m], xrecv.at[2, m, src], to_fore)
        over_sources(k, 2, one)

    def to_sibling(m, src):
        block = wbuf.at[m, src, pl.ds(base, nx)]
        send(block, block, ssend.at[m], srecv.at[m, src], to_core)

    def f_event(k, m):
        def one(src, way):
            arrived(wbuf.at[m, src, of_fore], xrecv.at[1, m, src])
            arrived(wbuf.at[m, src, of_far], xrecv.at[2, m, src])
            to_sibling(m, src)
        over_sources(k, 2, one)

    def rest_event(m):
        def one(src, way):
            arrived(wbuf.at[m, src, pl.ds(0, nx - 1)], zrest.at[m, way])
            to_sibling(m, src)
        over_sources(1, 1, one)

    def add_source(m, src):
        depth = width // nz
        at = pl.ds(pl.multiple_of(src * depth, HEAD_DIM), depth)
        acc[m] += dot(normed[:, at], wbuf[m, src].reshape(depth, cols))

    def use(m, src):
        arrived(wbuf.at[m, src, pl.ds(base, nx)], srecv.at[m, src])
        add_source(m, src)

    def g_event(k, least):
        over_sources(k, least, lambda src, way: use(2, src))

    def slot(t):
        for m in range(3):
            z_event(t - OFFSETS[m], m)
        for m in range(3):
            x_event(t - OFFSETS[m] - LAG_X, m)
        for m in range(3):
            f_event(t - OFFSETS[m] - LAG_F, m)
        g_event(t - OFFSETS[2] - LAG_G, 2)
        token_event(t)

    def slots(first, end, extra=None):
        @pl.loop(first, end)
        def _(t):
            slot(t)
            if extra is not None:
                extra(t - first)

    norm_rows = rows // 6 if rows % 96 == 0 else rows // 2

    def norm_block(i):
        at = pl.ds(pl.multiple_of(i * norm_rows, norm_rows), norm_rows)
        values = latents[at, :].astype(jnp.float32)
        center = values - jnp.mean(values, axis=-1, keepdims=True)
        spread = jnp.mean(center * center, axis=-1, keepdims=True)
        scaled = center * lax.rsqrt(spread + 1e-06) * modulation[1:2, :] + modulation[0:1, :]
        normed[at, :] = scaled.astype(jnp.bfloat16)

    def project(m):
        @pl.loop(0, nz)
        def _(src):
            pl.when(src == r)(lambda: add_source(m, src))
            pl.when(src != r)(lambda: use(m, src))

    def send_sums(i, values):
        wide = values.astype(jnp.float32)
        square = dot(jnp.ones((8, cols), jnp.float32), wide * wide, ((1,), (1,)), lax.Precision.HIGHEST)
        sums[i, tp] = jnp.zeros(sums.shape[2:], jnp.float32)
        sums[i, tp, :, 0:rows] = square[0:1]
        for j in range(1, nt):
            send(sums.at[i, tp], sums.at[i, tp], sumsend.at[i], sumrecv.at[i], {"tp": (tp + j) % nt})

    def inverse_rms(i):
        arrived(sums.at[i, pl.ds(0, nt - 1)], sumrecv.at[i])
        total = sums[i, 0]
        for j in range(1, nt):
            total = total + sums[i, j]
        return lax.rsqrt(total * (1.0 / (nt * cols)) + 1e-06)

    def gain_of(gain_ref):
        return gain_ref[:, pl.ds(pl.multiple_of(tp * cols, HEAD_DIM), cols)]

    def share_key_scale():
        scales[mine] = inverse_rms(0)
        for j in range(1, 2 * nx):
            send(scales.at[mine], scales.at[mine], scalesend, scalerecv, {"sp": (s + j) % (2 * nx)})

    def key_scale():
        arrived(scales.at[pl.ds(0, 2 * nx - 1)], scalerecv)
        for j in range(2 * nx):
            scale_row[:, j * rows : (j + 1) * rows] = scales[j, :, 0:rows]

    def normalise_query():
        scale = inverse_rms(1)
        column = jnp.concatenate(
            [jnp.transpose(jnp.broadcast_to(scale[:, j : j + 128], (128, 128))) for j in range(0, scale.shape[1], 128)],
            axis=0,
        )[0:rows]
        wide = qbuf[...].astype(jnp.float32) * gain_of(qgain_ref)
        parts = [wide[:, h * 128 : (h + 1) * 128] * column for h in range(heads)]
        qbuf[...] = jnp.concatenate(parts, axis=1).astype(jnp.bfloat16)

    def kv_send(j):
        block = kvbuf.at[j, mine]
        send(block, block, xsend.at[3 + j], kvrecv.at[0, j], to_fore)
        send(block, block, xsend.at[3 + j], kvrecv.at[1, j], to_back)
        send(block, block, ssend.at[3 + j], kvsib.at[j], to_core)

    def kv_pass(j):
        block = kvbuf.at[j, of_back]
        arrived(block, kvrecv.at[0, j])
        send(block, block, xsend.at[3 + j], kvrecv.at[2, j], to_fore)
        send(block, block, ssend.at[3 + j], kvsib.at[j], to_core)

    def kv_far(j):
        for kind, piece in ((1, of_fore), (2, of_far)):
            block = kvbuf.at[j, piece]
            arrived(block, kvrecv.at[kind, j])
            send(block, block, ssend.at[3 + j], kvsib.at[j], to_core)

    send_own(0)
    send_own(1)
    send_rest(0)
    acc[...] = jnp.zeros_like(acc)
    loads[1].wait()
    modulation[...] = table[steps_ref[0]]
    modulation[1:2, :] = modulation[1:2, :] + 1.0
    loads[0].wait()

    def early(i):
        norm_block(i)
        pl.when(i == OFFSETS[2] - 1)(lambda: send_own(2))
        pl.when(i == REST_1)(lambda: send_rest(1))

    done = 1 + rows // norm_rows
    slots(1, done, early)
    for load in loads[2:]:
        load.wait()
    add_source(2, r)
    ends = [nz + at + LAG_F for at in OFFSETS]
    rest_event(0)
    slots(done, REST_2)
    send_rest(2)
    slots(REST_2, ends[0])
    project(0)
    keys = acc[0].astype(jnp.bfloat16)
    kvbuf[0, mine] = (keys.astype(jnp.float32) * gain_of(kgain_ref)).astype(jnp.bfloat16)
    kv_send(0)
    send_sums(0, keys)
    rest_event(1)
    slots(ends[0], ends[1])
    project(1)
    qbuf[...] = acc[1].astype(jnp.bfloat16)
    send_sums(1, qbuf[...])
    kv_pass(0)
    rest_event(2)
    slots(ends[1], ends[2] - 1)
    kv_far(0)
    g_event(1, 1)
    slots(ends[2] - 1, ends[2])
    share_key_scale()
    slots(ends[2], nz + OFFSETS[2] + LAG_G)
    kvbuf[1, mine] = acc[2].astype(jnp.bfloat16)
    kv_send(1)
    normalise_query()
    key_scale()
    kv_pass(1)
    arrived(kvbuf.at[0, pl.ds(0, nx)], kvsib.at[0])

    inverse_root = 1.0 / HEAD_DIM**0.5
    keys_all = 2 * nx * rows
    totals = []
    for h in range(heads):
        at = slice(h * HEAD_DIM, (h + 1) * HEAD_DIM)
        scores = dot(qbuf[:, at], kvbuf[0, :, :, at].reshape(keys_all, HEAD_DIM), ((1,), (1,))) * (scale_row[...] * inverse_root)
        weights = jnp.exp(scores - jnp.max(scores, axis=-1, keepdims=True))
        totals.append(jnp.sum(weights, axis=-1, keepdims=True))
        probs[h] = weights.astype(jnp.bfloat16)
        if h == 0:
            kv_far(1)
    arrived(kvbuf.at[1, pl.ds(0, nx)], kvsib.at[1])
    for h in range(heads):
        at = slice(h * HEAD_DIM, (h + 1) * HEAD_DIM)
        context = dot(probs[h], kvbuf[1, :, :, at].reshape(keys_all, HEAD_DIM)) / totals[h]
        out_ref[:, at] = context.astype(jnp.bfloat16)

    inside = jnp.logical_and(r > 0, r < nz - 1)

    def pieces(m, count):
        outer = max(a for a in range(1, nz + 1) if count % a == 0 and count // a <= 2 * nx)
        return wbuf.at[m, pl.ds(0, outer), pl.ds(0, count // outer)]

    def wait_sends(z_count, x_count):
        for m in range(3):
            sent(pieces(m, z_count), zsend.at[m])
            sent(pieces(m, x_count), xsend.at[m])

    pl.when(inside)(lambda: wait_sends(2 * nx + nz - 1, 3 * (nz - 3)))
    pl.when(jnp.logical_not(inside))(lambda: wait_sends(nx, 3 * (nz - 2)))
    for m in range(3):
        sent(wbuf.at[m, pl.ds(0, nz - 1), pl.ds(0, nx)], ssend.at[m])
    for j in range(2):
        sent(kvbuf.at[j, pl.ds(0, 3)], xsend.at[3 + j])
        sent(kvbuf.at[j, pl.ds(0, nx)], ssend.at[3 + j])
        sent(sums.at[j, pl.ds(0, nt - 1)], sumsend.at[j])
    sent(scales.at[pl.ds(0, 2 * nx - 1)], scalesend)


def local(sizes, latents, timesteps, mod_table, w_query, w_key, w_value, q_gain, k_gain):
    nz, nx, nt = sizes
    rows, width = latents.shape[2:]
    cols = w_query.shape[1]
    part = w_query.shape[0] // (2 * nx)
    hbm, vmem = pl.BlockSpec(memory_space=pl.ANY), pl.BlockSpec(memory_space=pltpu.VMEM)
    split = [w.reshape(2 * nx, part, cols) for w in (w_key, w_query, w_value)]
    dma = pltpu.SemaphoreType.DMA
    out = pl.pallas_call(
        functools.partial(kernel, sizes),
        out_shape=jax.ShapeDtypeStruct((rows, cols), jnp.bfloat16),
        in_specs=[pl.BlockSpec(memory_space=pltpu.SMEM), hbm, hbm, hbm, hbm, hbm, vmem, vmem],
        out_specs=vmem,
        scratch_shapes=[
            pltpu.VMEM((3, nz, 2 * nx, part, cols), jnp.bfloat16),
            pltpu.VMEM((rows, width), jnp.bfloat16),
            pltpu.VMEM(mod_table.shape, jnp.float32),
            pltpu.VMEM((2, width), jnp.float32),
            pltpu.VMEM((rows, width), jnp.bfloat16),
            pltpu.VMEM((3, rows, cols), jnp.float32),
            pltpu.VMEM((2, 2 * nx, rows, cols), jnp.bfloat16),
            pltpu.VMEM((rows, cols), jnp.bfloat16),
            pltpu.VMEM((cols // HEAD_DIM, rows, 2 * nx * rows), jnp.bfloat16),
            pltpu.VMEM((2, nt, 1, (rows + 127) // 128 * 128), jnp.float32),
            pltpu.VMEM((2 * nx, 1, (rows + 127) // 128 * 128), jnp.float32),
            pltpu.VMEM((1, 2 * nx * rows), jnp.float32),
            pltpu.SemaphoreType.REGULAR,
            dma((5,)),
            dma((3, nz)),
            dma((3, 2)),
            dma((3, 3, nz)),
            dma((3, nz)),
            dma((3, 2)),
            dma((2,)),
            dma((2,)),
            dma,
            dma((3,)),
            dma((5,)),
            dma((5,)),
            dma((2,)),
            dma,
        ],
        compiler_params=pltpu.CompilerParams(
            collective_id=0, has_side_effects=True, vmem_limit_bytes=62 * 1024 * 1024
        ),
    )(
        timesteps,
        latents.reshape(rows, width),
        mod_table,
        *split,
        k_gain.reshape(1, -1),
        q_gain.reshape(1, -1),
    )
    return out.reshape(1, 1, rows, cols)


def solution(mesh):
    sizes = (mesh.shape["rep"], mesh.shape["sp"] // 2, mesh.shape["tp"])
    return jax.shard_map(
        functools.partial(local, sizes),
        mesh=mesh,
        in_specs=(
            P("rep", None, "sp", None),
            P("rep"),
            P(),
            P("rep", "tp"),
            P("rep", "tp"),
            P("rep", "tp"),
            P(),
            P(),
        ),
        out_specs=P("rep", None, "sp", "tp"),
        check_vma=False,
    )
```

```python
import functools

import jax
import jax.numpy as jnp
from jax import lax
from jax.experimental import pallas as pl
from jax.experimental.pallas import tpu as pltpu
from jax.sharding import PartitionSpec as P

HEAD_DIM = 128
OFFSETS = (0, 1, 3)
PAIRS = (False, False, True)
LAG_X = 1
LAG_F = 2
LAG_G = 3
MESH = pl.DeviceIdType.MESH


def dot(a, b, dims=((1,), (0,)), precision=None):
    return lax.dot_general(a, b, (dims, ((), ())), precision=precision, preferred_element_type=jnp.float32)


def kernel(
    sizes,
    steps_ref, latents_hbm, table_hbm, wk_hbm, wq_hbm, wv_hbm, kgain_ref, qgain_ref,
    out_ref,
    wbuf, latents, table, modulation, normed, acc, kvbuf, qbuf, probs, sums, scales, knbuf, answered,
    local_sem, zrecv, zfar, xrecv, srecv, kvrecv, kvsib, sumrecv, scalerecv, zsend, xsend, ssend, sumsend, scalesend,
):
    nz, nx, nt = sizes
    r, s, tp = lax.axis_index("rep"), lax.axis_index("sp"), lax.axis_index("tp")
    x, c = s // 2, s % 2
    step = 1 - 2 * c
    fore, back = (x + step + nx) % nx, (x - step + nx) % nx
    base = c * nx
    mine, of_back, of_fore, of_far = base + x, base + back, base + fore, base + (x + 2) % nx
    to_fore, to_back, to_core = {"sp": fore * 2 + c}, {"sp": back * 2 + c}, {"sp": s + 1 - 2 * c}
    up, down = {"rep": r + 1}, {"rep": r - 1}
    whbm = (wk_hbm, wq_hbm, wv_hbm)
    rows, width = latents.shape
    cols = kvbuf.shape[3]
    heads = cols // HEAD_DIM

    def send(src, dst, send_sem, recv_sem, where):
        pltpu.make_async_remote_copy(src, dst, send_sem, recv_sem, device_id=where, device_id_type=MESH).start()

    def arrived(ref, recv_sem):
        pltpu.make_async_remote_copy(ref, ref, xsend.at[0], recv_sem, device_id=to_fore, device_id_type=MESH).wait_recv()

    def sent(ref, send_sem):
        pltpu.make_async_remote_copy(ref, ref, send_sem, sumrecv.at[0], device_id=to_fore, device_id_type=MESH).wait_send()

    loads = [pltpu.make_async_copy(latents_hbm, latents, local_sem.at[0]),
             pltpu.make_async_copy(table_hbm, table, local_sem.at[1])]
    loads += [pltpu.make_async_copy(whbm[m], wbuf.at[m, r], local_sem.at[2 + m]) for m in range(3)]
    for load in loads:
        load.start()

    barrier = pltpu.get_barrier_semaphore()

    def greet(where):
        pl.semaphore_signal(barrier, inc=1, device_id=where, device_id_type=MESH)

    ny = nt // 2
    lower = tp < ny

    def far_peers(action):
        for i in range(ny):
            action({"tp": (tp + ny) % nt // ny * ny + i})

    for where in (to_fore, to_back, to_core):
        greet(where)
    pl.when(r < nz - 1)(lambda: greet(up))
    pl.when(r > 0)(lambda: greet(down))
    for i in range(1, ny):
        greet({"tp": (tp // ny) * ny + (tp + i) % ny})
    pl.when(lower)(lambda: far_peers(greet))
    at_end = jnp.logical_or(r == 0, r == nz - 1)

    def wait_greetings(near):
        pl.when(lower)(lambda: pl.semaphore_wait(barrier, near))
        pl.when(jnp.logical_not(lower))(lambda: pl.semaphore_wait(barrier, near + ny))

    pl.when(at_end)(lambda: wait_greetings(3 + ny))
    pl.when(jnp.logical_not(at_end))(lambda: wait_greetings(4 + ny))

    def answer(where):
        pl.semaphore_signal(answered, inc=1, device_id=where, device_id_type=MESH)

    pl.when(jnp.logical_not(lower))(lambda: far_peers(answer))

    def both_ways(action):
        pl.when(r < nz - 1)(lambda: action(up, 0))
        pl.when(r > 0)(lambda: action(down, 1))

    def send_own(m):
        def one(where, way):
            send(whbm[m].at[mine], wbuf.at[m, r, mine], zsend.at[m], zrecv.at[m, r], where)
            if PAIRS[m]:
                send(whbm[m].at[of_far], wbuf.at[m, r, of_far], zsend.at[m], zfar.at[m, r], where)
        both_ways(one)

    def over_sources(k, least, action):
        pl.when(jnp.logical_and(k >= least, r - k >= 0))(lambda: action(r - k, 0))
        pl.when(jnp.logical_and(k >= least, r + k <= nz - 1))(lambda: action(r + k, 1))

    def z_event(k, m):
        def one(src, way):
            def pass_on(place, sems):
                piece = wbuf.at[m, src, place]
                arrived(piece, sems.at[m, src])
                if way == 0:
                    pl.when(r < nz - 1)(lambda: send(piece, piece, zsend.at[m], sems.at[m, src], up))
                else:
                    pl.when(r > 0)(lambda: send(piece, piece, zsend.at[m], sems.at[m, src], down))

            pass_on(mine, zrecv)
            piece = wbuf.at[m, src, mine]
            send(piece, piece, xsend.at[m], xrecv.at[0, m, src], to_fore)
            send(piece, piece, xsend.at[m], xrecv.at[1, m, src], to_back)
            if PAIRS[m]:
                pass_on(of_far, zfar)
        over_sources(k, 1, one)

    upper = r // (nz // 2)
    edge = r + upper * (nz - 1 - 2 * r)

    def nth_source(n, action):
        @pl.when(jnp.logical_and(n >= 1, n <= nz - 1))
        def _():
            both = n <= 2 * edge
            sign = jnp.where(both, 2 * ((n - 1) % 2) - 1, 1 - 2 * upper)
            action(r + sign * jnp.where(both, (n + 1) // 2, n - edge))

    def x_event(n, m):
        if PAIRS[m]:
            return

        def one(src):
            piece = wbuf.at[m, src, of_back]
            arrived(piece, xrecv.at[0, m, src])
            send(piece, piece, xsend.at[m], xrecv.at[2, m, src], to_fore)
        nth_source(n, one)

    def to_sibling(m, src):
        block = wbuf.at[m, src, pl.ds(base, nx)]
        send(block, block, ssend.at[m], srecv.at[m, src], to_core)

    def f_event(n, m):
        def one(src):
            arrived(wbuf.at[m, src, of_fore], xrecv.at[1, m, src])
            if PAIRS[m]:
                arrived(wbuf.at[m, src, of_back], xrecv.at[0, m, src])
            else:
                arrived(wbuf.at[m, src, of_far], xrecv.at[2, m, src])
            to_sibling(m, src)
        nth_source(n, one)

    def add_source(m, src):
        depth = width // nz
        at = pl.ds(pl.multiple_of(src * depth, HEAD_DIM), depth)
        acc[m] += dot(normed[:, at], wbuf[m, src].reshape(depth, cols))

    def use(m, src):
        arrived(wbuf.at[m, src, pl.ds(base, nx)], srecv.at[m, src])
        add_source(m, src)

    def g_event(n):
        nth_source(n, lambda src: use(2, src))

    def slot(t):
        for m in range(3):
            z_event(t - OFFSETS[m], m)
        for m in range(3):
            x_event(t - OFFSETS[m] - LAG_X, m)
        for m in range(3):
            f_event(t - OFFSETS[m] - LAG_F, m)
        g_event(t - OFFSETS[2] - LAG_G)

    def slots(first, end, extra=None):
        @pl.loop(first, end)
        def _(t):
            slot(t)
            if extra is not None:
                extra(t - first)

    norm_rows = rows // 6 if rows % 96 == 0 else rows // 2

    def norm_block(i):
        at = pl.ds(pl.multiple_of(i * norm_rows, norm_rows), norm_rows)
        values = latents[at, :].astype(jnp.float32)
        center = values - jnp.mean(values, axis=-1, keepdims=True)
        spread = jnp.mean(center * center, axis=-1, keepdims=True)
        scaled = center * lax.rsqrt(spread + 1e-06) * modulation[1:2, :] + modulation[0:1, :]
        normed[at, :] = scaled.astype(jnp.bfloat16)

    def project(m):
        @pl.loop(0, nz)
        def _(src):
            pl.when(src == r)(lambda: add_source(m, src))
            pl.when(src != r)(lambda: use(m, src))

    def send_sums(i, values):
        wide = values.astype(jnp.float32)
        square = dot(jnp.ones((8, cols), jnp.float32), wide * wide, ((1,), (1,)), lax.Precision.HIGHEST)
        sums[i, tp] = jnp.zeros(sums.shape[2:], jnp.float32)
        sums[i, tp, :, 0:rows] = square[0:1]
        for j in range(1, nt):
            send(sums.at[i, tp], sums.at[i, tp], sumsend.at[i], sumrecv.at[i], {"tp": (tp + j) % nt})

    def inverse_rms(i):
        arrived(sums.at[i, pl.ds(0, nt - 1)], sumrecv.at[i])
        total = sums[i, 0]
        for j in range(1, nt):
            total = total + sums[i, j]
        return lax.rsqrt(total * (1.0 / (nt * cols)) + 1e-06)

    def gain_of(gain_ref):
        return gain_ref[:, pl.ds(pl.multiple_of(tp * cols, HEAD_DIM), cols)]

    def share_key_scale():
        scales[mine] = inverse_rms(0)
        for j in range(1, 2 * nx):
            send(scales.at[mine], scales.at[mine], scalesend, scalerecv, {"sp": (s + j) % (2 * nx)})

    def normalise(values, scale, gain_ref):
        column = jnp.concatenate(
            [jnp.transpose(jnp.broadcast_to(scale[:, j : j + 128], (128, 128))) for j in range(0, scale.shape[1], 128)],
            axis=0,
        )[0:rows]
        wide = values.astype(jnp.float32) * gain_of(gain_ref)
        parts = [wide[:, h * 128 : (h + 1) * 128] * column for h in range(heads)]
        return jnp.concatenate(parts, axis=1).astype(jnp.bfloat16)

    def normalise_keys():
        arrived(scales.at[pl.ds(0, 2 * nx - 1)], scalerecv)

        @pl.loop(0, 2 * nx)
        def _(j):
            knbuf[j] = normalise(kvbuf[0, j], scales[j], kgain_ref)

    def kv_send(j):
        block = kvbuf.at[j, mine]
        send(block, block, xsend.at[3 + j], kvrecv.at[0, j], to_fore)
        send(block, block, xsend.at[3 + j], kvrecv.at[1, j], to_back)
        send(block, block, ssend.at[3 + j], kvsib.at[j], to_core)
        if j == 1:
            send(block, block, xsend.at[3 + j], kvrecv.at[2, j], {"sp": (x + 2) % nx * 2 + c})

    def kv_pass(j):
        block = kvbuf.at[j, of_back]
        arrived(block, kvrecv.at[0, j])
        if j == 0:
            send(block, block, xsend.at[3 + j], kvrecv.at[2, j], to_fore)
        send(block, block, ssend.at[3 + j], kvsib.at[j], to_core)

    def kv_far(j):
        for kind, piece in ((1, of_fore), (2, of_far)):
            block = kvbuf.at[j, piece]
            arrived(block, kvrecv.at[kind, j])
            send(block, block, ssend.at[3 + j], kvsib.at[j], to_core)

    send_own(0)
    send_own(1)
    acc[...] = jnp.zeros_like(acc)
    loads[1].wait()
    modulation[...] = table[steps_ref[0]]
    modulation[1:2, :] = modulation[1:2, :] + 1.0
    loads[0].wait()

    def early(i):
        norm_block(i)
        pl.when(i == OFFSETS[2] - 1)(lambda: send_own(2))

    done = 1 + rows // norm_rows
    slots(1, done, early)
    for load in loads[2:]:
        load.wait()
    add_source(2, r)
    ends = [nz + at + LAG_F for at in OFFSETS]
    slots(done, ends[0])
    project(0)
    kvbuf[0, mine] = acc[0].astype(jnp.bfloat16)
    kv_send(0)
    pl.when(lower)(lambda: pl.semaphore_wait(answered, ny))
    send_sums(0, kvbuf[0, mine])
    slots(ends[0], ends[1])
    project(1)
    qbuf[...] = acc[1].astype(jnp.bfloat16)
    send_sums(1, qbuf[...])
    kv_pass(0)
    slots(ends[1], ends[2] - 1)
    kv_far(0)
    slots(ends[2] - 1, ends[2])
    share_key_scale()
    slots(ends[2], nz + OFFSETS[2] + LAG_G)
    kvbuf[1, mine] = acc[2].astype(jnp.bfloat16)
    kv_send(1)
    arrived(kvbuf.at[0, pl.ds(0, nx)], kvsib.at[0])
    normalise_keys()
    qbuf[...] = normalise(qbuf[...], inverse_rms(1), qgain_ref)

    inverse_root = 1.0 / HEAD_DIM**0.5
    keys_all = 2 * nx * rows
    totals = []
    for h in range(heads):
        at = slice(h * HEAD_DIM, (h + 1) * HEAD_DIM)
        scores = dot(qbuf[:, at], knbuf[:, :, at].reshape(keys_all, HEAD_DIM), ((1,), (1,))) * inverse_root
        weights = jnp.exp(scores - jnp.max(scores, axis=-1, keepdims=True))
        totals.append(jnp.sum(weights, axis=-1, keepdims=True))
        probs[h] = weights.astype(jnp.bfloat16)
        if h == 0:
            kv_pass(1)
            kv_far(1)
    arrived(kvbuf.at[1, pl.ds(0, nx)], kvsib.at[1])
    for h in range(heads):
        at = slice(h * HEAD_DIM, (h + 1) * HEAD_DIM)
        context = dot(probs[h], kvbuf[1, :, :, at].reshape(keys_all, HEAD_DIM)) / totals[h]
        out_ref[:, at] = context.astype(jnp.bfloat16)


    def pieces(m, count):
        outer = max(a for a in range(1, nz + 1) if count % a == 0 and count // a <= 2 * nx)
        return wbuf.at[m, pl.ds(0, outer), pl.ds(0, count // outer)]

    def wait_sends(count):
        for m in range(3):
            sent(pieces(m, count * (2 if PAIRS[m] else 1)), zsend.at[m])

    pl.when(edge > 0)(lambda: wait_sends(nz + 1))
    pl.when(edge == 0)(lambda: wait_sends(1))
    for m in range(3):
        sent(pieces(m, (nz - 1) * (2 if PAIRS[m] else 3)), xsend.at[m])
    for m in range(3):
        sent(wbuf.at[m, pl.ds(0, nz - 1), pl.ds(0, nx)], ssend.at[m])
    for j in range(2):
        sent(kvbuf.at[j, pl.ds(0, 3)], xsend.at[3 + j])
        sent(kvbuf.at[j, pl.ds(0, nx)], ssend.at[3 + j])
        sent(sums.at[j, pl.ds(0, nt - 1)], sumsend.at[j])
    sent(scales.at[pl.ds(0, 2 * nx - 1)], scalesend)


def local(sizes, latents, timesteps, mod_table, w_query, w_key, w_value, q_gain, k_gain):
    nz, nx, nt = sizes
    rows, width = latents.shape[2:]
    cols = w_query.shape[1]
    part = w_query.shape[0] // (2 * nx)
    hbm, vmem = pl.BlockSpec(memory_space=pl.ANY), pl.BlockSpec(memory_space=pltpu.VMEM)
    split = [w.reshape(2 * nx, part, cols) for w in (w_key, w_query, w_value)]
    dma = pltpu.SemaphoreType.DMA
    out = pl.pallas_call(
        functools.partial(kernel, sizes),
        out_shape=jax.ShapeDtypeStruct((rows, cols), jnp.bfloat16),
        in_specs=[pl.BlockSpec(memory_space=pltpu.SMEM), hbm, hbm, hbm, hbm, hbm, vmem, vmem],
        out_specs=vmem,
        scratch_shapes=[
            pltpu.VMEM((3, nz, 2 * nx, part, cols), jnp.bfloat16),
            pltpu.VMEM((rows, width), jnp.bfloat16),
            pltpu.VMEM(mod_table.shape, jnp.float32),
            pltpu.VMEM((2, width), jnp.float32),
            pltpu.VMEM((rows, width), jnp.bfloat16),
            pltpu.VMEM((3, rows, cols), jnp.float32),
            pltpu.VMEM((2, 2 * nx, rows, cols), jnp.bfloat16),
            pltpu.VMEM((rows, cols), jnp.bfloat16),
            pltpu.VMEM((cols // HEAD_DIM, rows, 2 * nx * rows), jnp.bfloat16),
            pltpu.VMEM((2, nt, 1, (rows + 127) // 128 * 128), jnp.float32),
            pltpu.VMEM((2 * nx, 1, (rows + 127) // 128 * 128), jnp.float32),
            pltpu.VMEM((2 * nx, rows, cols), jnp.bfloat16),
            pltpu.SemaphoreType.REGULAR,
            dma((5,)),
            dma((3, nz)),
            dma((3, nz)),
            dma((3, 3, nz)),
            dma((3, nz)),
            dma((3, nz)),
            dma((2,)),
            dma((2,)),
            dma,
            dma((3,)),
            dma((5,)),
            dma((5,)),
            dma((2,)),
            dma,
        ],
        compiler_params=pltpu.CompilerParams(
            collective_id=0, has_side_effects=True, vmem_limit_bytes=62 * 1024 * 1024
        ),
    )(
        timesteps,
        latents.reshape(rows, width),
        mod_table,
        *split,
        k_gain.reshape(1, -1),
        q_gain.reshape(1, -1),
    )
    return out.reshape(1, 1, rows, cols)


def solution(mesh):
    sizes = (mesh.shape["rep"], mesh.shape["sp"] // 2, mesh.shape["tp"])
    return jax.shard_map(
        functools.partial(local, sizes),
        mesh=mesh,
        in_specs=(
            P("rep", None, "sp", None),
            P("rep"),
            P(),
            P("rep", "tp"),
            P("rep", "tp"),
            P("rep", "tp"),
            P(),
            P(),
        ),
        out_specs=P("rep", None, "sp", "tp"),
        check_vma=False,
    )
```

```python
import functools

import jax
import jax.numpy as jnp
from jax import lax
from jax.experimental import pallas as pl
from jax.experimental.pallas import tpu as pltpu
from jax.sharding import PartitionSpec as P

HEAD_DIM = 128
OFFSETS = (0, 1, 2, 3)
PAIRS = (False, False, True, True)
LAG_X = 1
LAG_F = 2
LAG_G = 3
MESH = pl.DeviceIdType.MESH


def dot(a, b, dims=((1,), (0,)), precision=None):
    return lax.dot_general(a, b, (dims, ((), ())), precision=precision, preferred_element_type=jnp.float32)


def kernel(
    sizes,
    steps_ref, latents_hbm, table_hbm, wk_hbm, wq_hbm, wv_hbm, kgain_ref, qgain_ref,
    out_ref,
    wbuf, latents, table, modulation, normed, acc, kvbuf, qbuf, probs, sums, scales, knbuf, answered,
    local_sem, zrecv, zfar, xrecv, srecv, kvrecv, kvsib, sumrecv, scalerecv, zsend, xsend, ssend, sumsend, scalesend,
):
    nz, nx, nt = sizes
    r, s, tp = lax.axis_index("rep"), lax.axis_index("sp"), lax.axis_index("tp")
    x, c = s // 2, s % 2
    step = 1 - 2 * c
    fore, back = (x + step + nx) % nx, (x - step + nx) % nx
    base = c * nx
    mine, of_back, of_fore, of_far = base + x, base + back, base + fore, base + (x + 2) % nx
    to_fore, to_back, to_core = {"sp": fore * 2 + c}, {"sp": back * 2 + c}, {"sp": s + 1 - 2 * c}
    up, down = {"rep": r + 1}, {"rep": r - 1}
    whbm = (wk_hbm, wq_hbm, wv_hbm)
    rows, width = latents.shape
    cols = kvbuf.shape[3]
    heads = cols // HEAD_DIM

    split = cols - HEAD_DIM
    streams = ((0, 0, cols), (1, 0, cols), (2, 0, split), (2, split, cols))
    count = len(streams)

    def weight(m, src, piece):
        which, first, end = streams[m]
        return wbuf.at[which, src, piece, :, pl.ds(first, end - first)]

    def own_weight(m, piece):
        which, first, end = streams[m]
        return whbm[which].at[piece, :, pl.ds(first, end - first)]

    shared = ((0, 0, cols), (1, 0, split), (1, split, cols))

    def kv_part(j, piece):
        which, first, end = shared[j]
        return kvbuf.at[which, piece, :, pl.ds(first, end - first)]

    def send(src, dst, send_sem, recv_sem, where):
        pltpu.make_async_remote_copy(src, dst, send_sem, recv_sem, device_id=where, device_id_type=MESH).start()

    def arrived(ref, recv_sem):
        pltpu.make_async_remote_copy(ref, ref, xsend.at[0], recv_sem, device_id=to_fore, device_id_type=MESH).wait_recv()

    def sent(ref, send_sem):
        pltpu.make_async_remote_copy(ref, ref, send_sem, sumrecv.at[0], device_id=to_fore, device_id_type=MESH).wait_send()

    loads = [pltpu.make_async_copy(latents_hbm, latents, local_sem.at[0]),
             pltpu.make_async_copy(table_hbm, table, local_sem.at[1])]
    loads += [pltpu.make_async_copy(whbm[m], wbuf.at[m, r], local_sem.at[2 + m]) for m in range(3)]
    for load in loads:
        load.start()

    barrier = pltpu.get_barrier_semaphore()

    def greet(where):
        pl.semaphore_signal(barrier, inc=1, device_id=where, device_id_type=MESH)

    ny = nt // 2
    lower = tp < ny

    def far_peers(action):
        for i in range(ny):
            action({"tp": (tp + ny) % nt // ny * ny + i})

    for where in (to_fore, to_back, to_core):
        greet(where)
    pl.when(r < nz - 1)(lambda: greet(up))
    pl.when(r > 0)(lambda: greet(down))
    for i in range(1, ny):
        greet({"tp": (tp // ny) * ny + (tp + i) % ny})
    pl.when(lower)(lambda: far_peers(greet))
    at_end = jnp.logical_or(r == 0, r == nz - 1)

    def wait_greetings(near):
        pl.when(lower)(lambda: pl.semaphore_wait(barrier, near))
        pl.when(jnp.logical_not(lower))(lambda: pl.semaphore_wait(barrier, near + ny))

    pl.when(at_end)(lambda: wait_greetings(3 + ny))
    pl.when(jnp.logical_not(at_end))(lambda: wait_greetings(4 + ny))

    def answer(where):
        pl.semaphore_signal(answered, inc=1, device_id=where, device_id_type=MESH)

    pl.when(jnp.logical_not(lower))(lambda: far_peers(answer))

    def both_ways(action):
        pl.when(r < nz - 1)(lambda: action(up, 0))
        pl.when(r > 0)(lambda: action(down, 1))

    def send_own(m):
        def one(where, way):
            send(own_weight(m, mine), weight(m, r, mine), zsend.at[m], zrecv.at[m, r], where)
            if PAIRS[m]:
                send(own_weight(m, of_far), weight(m, r, of_far), zsend.at[m], zfar.at[m, r], where)
        both_ways(one)

    def over_sources(k, least, action):
        pl.when(jnp.logical_and(k >= least, r - k >= 0))(lambda: action(r - k, 0))
        pl.when(jnp.logical_and(k >= least, r + k <= nz - 1))(lambda: action(r + k, 1))

    def z_event(k, m):
        def one(src, way):
            def pass_on(place, sems):
                piece = weight(m, src, place)
                arrived(piece, sems.at[m, src])
                if way == 0:
                    pl.when(r < nz - 1)(lambda: send(piece, piece, zsend.at[m], sems.at[m, src], up))
                else:
                    pl.when(r > 0)(lambda: send(piece, piece, zsend.at[m], sems.at[m, src], down))

            pass_on(mine, zrecv)
            piece = weight(m, src, mine)
            send(piece, piece, xsend.at[m], xrecv.at[0, m, src], to_fore)
            send(piece, piece, xsend.at[m], xrecv.at[1, m, src], to_back)
            if PAIRS[m]:
                pass_on(of_far, zfar)
        over_sources(k, 1, one)

    upper = r // (nz // 2)
    edge = r + upper * (nz - 1 - 2 * r)

    def nth_source(n, action):
        @pl.when(jnp.logical_and(n >= 1, n <= nz - 1))
        def _():
            both = n <= 2 * edge
            sign = jnp.where(both, 2 * ((n - 1) % 2) - 1, 1 - 2 * upper)
            action(r + sign * jnp.where(both, (n + 1) // 2, n - edge))

    def x_event(n, m):
        if PAIRS[m]:
            return

        def one(src):
            piece = weight(m, src, of_back)
            arrived(piece, xrecv.at[0, m, src])
            send(piece, piece, xsend.at[m], xrecv.at[2, m, src], to_fore)
        nth_source(n, one)

    def to_sibling(m, src):
        block = weight(m, src, pl.ds(base, nx))
        send(block, block, ssend.at[m], srecv.at[m, src], to_core)

    def f_event(n, m):
        def one(src):
            arrived(weight(m, src, of_fore), xrecv.at[1, m, src])
            if PAIRS[m]:
                arrived(weight(m, src, of_back), xrecv.at[0, m, src])
            else:
                arrived(weight(m, src, of_far), xrecv.at[2, m, src])
            to_sibling(m, src)
        nth_source(n, one)

    def add_source(m, src):
        depth = width // nz
        at = pl.ds(pl.multiple_of(src * depth, HEAD_DIM), depth)
        which, first, end = streams[m]
        acc[which, :, first:end] += dot(normed[:, at], wbuf[which, src, :, :, first:end].reshape(depth, end - first))

    def use(m, src):
        arrived(weight(m, src, pl.ds(base, nx)), srecv.at[m, src])
        add_source(m, src)

    def g_event(n, m):
        nth_source(n, lambda src: use(m, src))

    def slot(t):
        for m in range(count):
            z_event(t - OFFSETS[m], m)
        for m in range(count):
            x_event(t - OFFSETS[m] - LAG_X, m)
        for m in range(count):
            f_event(t - OFFSETS[m] - LAG_F, m)
        for m in range(2, count):
            g_event(t - OFFSETS[m] - LAG_G, m)

    def slots(first, end, extra=None):
        @pl.loop(first, end)
        def _(t):
            slot(t)
            if extra is not None:
                extra(t - first)

    norm_rows = rows // 4

    def norm_block(i):
        at = pl.ds(pl.multiple_of(i * norm_rows, norm_rows), norm_rows)
        values = latents[at, :].astype(jnp.float32)
        center = values - jnp.mean(values, axis=-1, keepdims=True)
        spread = jnp.mean(center * center, axis=-1, keepdims=True)
        scaled = center * lax.rsqrt(spread + 1e-06) * modulation[1:2, :] + modulation[0:1, :]
        normed[at, :] = scaled.astype(jnp.bfloat16)

    def project(m):
        @pl.loop(0, nz)
        def _(src):
            pl.when(src == r)(lambda: add_source(m, src))
            pl.when(src != r)(lambda: use(m, src))

    def send_sums(i, values):
        wide = values.astype(jnp.float32)
        square = dot(jnp.ones((8, cols), jnp.float32), wide * wide, ((1,), (1,)), lax.Precision.HIGHEST)
        sums[i, tp] = jnp.zeros(sums.shape[2:], jnp.float32)
        sums[i, tp, :, 0:rows] = square[0:1]
        for j in range(1, nt):
            send(sums.at[i, tp], sums.at[i, tp], sumsend.at[i], sumrecv.at[i], {"tp": (tp + j) % nt})

    def inverse_rms(i):
        arrived(sums.at[i, pl.ds(0, nt - 1)], sumrecv.at[i])
        total = sums[i, 0]
        for j in range(1, nt):
            total = total + sums[i, j]
        return lax.rsqrt(total * (1.0 / (nt * cols)) + 1e-06)

    def gain_of(gain_ref):
        return gain_ref[:, pl.ds(pl.multiple_of(tp * cols, HEAD_DIM), cols)]

    def share_key_scale():
        scales[mine] = inverse_rms(0)
        for j in range(1, 2 * nx):
            send(scales.at[mine], scales.at[mine], scalesend, scalerecv, {"sp": (s + j) % (2 * nx)})

    def normalise(values, scale, gain_ref):
        column = jnp.concatenate(
            [jnp.transpose(jnp.broadcast_to(scale[:, j : j + 128], (128, 128))) for j in range(0, scale.shape[1], 128)],
            axis=0,
        )[0:rows]
        wide = values.astype(jnp.float32) * gain_of(gain_ref)
        parts = [wide[:, h * 128 : (h + 1) * 128] * column for h in range(heads)]
        return jnp.concatenate(parts, axis=1).astype(jnp.bfloat16)

    def normalise_keys():
        arrived(scales.at[pl.ds(0, 2 * nx - 1)], scalerecv)

        @pl.loop(0, 2 * nx)
        def _(j):
            knbuf[j] = normalise(kvbuf[0, j], scales[j], kgain_ref)

    def kv_send(j):
        block = kv_part(j, mine)
        send(block, block, xsend.at[count + j], kvrecv.at[0, j], to_fore)
        send(block, block, xsend.at[count + j], kvrecv.at[1, j], to_back)
        if j > 0:
            send(block, block, xsend.at[count + j], kvrecv.at[2, j], {"sp": (x + 2) % nx * 2 + c})
        send(block, block, ssend.at[count + j], kvsib.at[j], to_core)

    def kv_pass(j):
        block = kv_part(j, of_back)
        arrived(block, kvrecv.at[0, j])
        if j == 0:
            send(block, block, xsend.at[count + j], kvrecv.at[2, j], to_fore)
        send(block, block, ssend.at[count + j], kvsib.at[j], to_core)

    def kv_far(j):
        for kind, piece in ((1, of_fore), (2, of_far)):
            block = kv_part(j, piece)
            arrived(block, kvrecv.at[kind, j])
            send(block, block, ssend.at[count + j], kvsib.at[j], to_core)

    send_own(0)
    send_own(1)
    acc[...] = jnp.zeros_like(acc)
    loads[1].wait()
    modulation[...] = table[steps_ref[0]]
    modulation[1:2, :] = modulation[1:2, :] + 1.0
    loads[0].wait()

    def early(i):
        norm_block(i)
        for m in range(2, count):
            pl.when(i == OFFSETS[m] - 1)(functools.partial(send_own, m))

    done = 1 + rows // norm_rows
    slots(1, done, early)
    for load in loads[2:]:
        load.wait()
    for m in range(2, count):
        add_source(m, r)
    ends = [nz + at + LAG_F for at in OFFSETS]
    slots(done, ends[0])
    project(0)
    kvbuf[0, mine] = acc[0].astype(jnp.bfloat16)
    kv_send(0)
    pl.when(lower)(lambda: pl.semaphore_wait(answered, ny))
    send_sums(0, kvbuf[0, mine])
    slots(ends[0], ends[1])
    project(1)
    qbuf[...] = acc[1].astype(jnp.bfloat16)
    send_sums(1, qbuf[...])
    kv_pass(0)
    slots(ends[1], ends[1] + 1)
    kv_far(0)
    slots(ends[1] + 1, ends[1] + 2)
    kvbuf[1, mine, :, 0:split] = acc[2, :, 0:split].astype(jnp.bfloat16)
    kv_send(1)
    share_key_scale()
    slots(ends[1] + 2, nz + OFFSETS[3] + LAG_G)
    kvbuf[1, mine, :, split:cols] = acc[2, :, split:cols].astype(jnp.bfloat16)
    kv_send(2)
    arrived(kv_part(0, pl.ds(0, nx)), kvsib.at[0])
    normalise_keys()
    qbuf[...] = normalise(qbuf[...], inverse_rms(1), qgain_ref)

    inverse_root = 1.0 / HEAD_DIM**0.5
    keys_all = 2 * nx * rows
    totals = []
    for h in range(heads):
        at = slice(h * HEAD_DIM, (h + 1) * HEAD_DIM)
        scores = dot(qbuf[:, at], knbuf[:, :, at].reshape(keys_all, HEAD_DIM), ((1,), (1,))) * inverse_root
        weights = jnp.exp(scores - jnp.max(scores, axis=-1, keepdims=True))
        totals.append(jnp.sum(weights, axis=-1, keepdims=True))
        probs[h] = weights.astype(jnp.bfloat16)
        if h < 2:
            kv_pass(1 + h)
            kv_far(1 + h)
    arrived(kv_part(1, pl.ds(0, nx)), kvsib.at[1])
    for h in range(heads):
        at = slice(h * HEAD_DIM, (h + 1) * HEAD_DIM)
        if h == heads - 1:
            arrived(kv_part(2, pl.ds(0, nx)), kvsib.at[2])
        context = dot(probs[h], kvbuf[1, :, :, at].reshape(keys_all, HEAD_DIM)) / totals[h]
        out_ref[:, at] = context.astype(jnp.bfloat16)


    def pieces(m, copies):
        outer = max(a for a in range(1, nz + 1) if copies % a == 0 and copies // a <= 2 * nx)
        return weight(m, pl.ds(0, outer), pl.ds(0, copies // outer))

    def wait_sends(copies):
        for m in range(count):
            sent(pieces(m, copies * (2 if PAIRS[m] else 1)), zsend.at[m])

    pl.when(edge > 0)(lambda: wait_sends(nz + 1))
    pl.when(edge == 0)(lambda: wait_sends(1))
    for m in range(count):
        sent(pieces(m, (nz - 1) * (2 if PAIRS[m] else 3)), xsend.at[m])
    for m in range(count):
        sent(weight(m, pl.ds(0, nz - 1), pl.ds(0, nx)), ssend.at[m])
    for j in range(3):
        sent(kv_part(j, pl.ds(0, 3)), xsend.at[count + j])
        sent(kv_part(j, pl.ds(0, nx)), ssend.at[count + j])
    for j in range(2):
        sent(sums.at[j, pl.ds(0, nt - 1)], sumsend.at[j])
    sent(scales.at[pl.ds(0, 2 * nx - 1)], scalesend)


def local(sizes, latents, timesteps, mod_table, w_query, w_key, w_value, q_gain, k_gain):
    nz, nx, nt = sizes
    rows, width = latents.shape[2:]
    cols = w_query.shape[1]
    part = w_query.shape[0] // (2 * nx)
    hbm, vmem = pl.BlockSpec(memory_space=pl.ANY), pl.BlockSpec(memory_space=pltpu.VMEM)
    split = [w.reshape(2 * nx, part, cols) for w in (w_key, w_query, w_value)]
    dma = pltpu.SemaphoreType.DMA
    out = pl.pallas_call(
        functools.partial(kernel, sizes),
        out_shape=jax.ShapeDtypeStruct((rows, cols), jnp.bfloat16),
        in_specs=[pl.BlockSpec(memory_space=pltpu.SMEM), hbm, hbm, hbm, hbm, hbm, vmem, vmem],
        out_specs=vmem,
        scratch_shapes=[
            pltpu.VMEM((3, nz, 2 * nx, part, cols), jnp.bfloat16),
            pltpu.VMEM((rows, width), jnp.bfloat16),
            pltpu.VMEM(mod_table.shape, jnp.float32),
            pltpu.VMEM((2, width), jnp.float32),
            pltpu.VMEM((rows, width), jnp.bfloat16),
            pltpu.VMEM((3, rows, cols), jnp.float32),
            pltpu.VMEM((2, 2 * nx, rows, cols), jnp.bfloat16),
            pltpu.VMEM((rows, cols), jnp.bfloat16),
            pltpu.VMEM((cols // HEAD_DIM, rows, 2 * nx * rows), jnp.bfloat16),
            pltpu.VMEM((2, nt, 1, (rows + 127) // 128 * 128), jnp.float32),
            pltpu.VMEM((2 * nx, 1, (rows + 127) // 128 * 128), jnp.float32),
            pltpu.VMEM((2 * nx, rows, cols), jnp.bfloat16),
            pltpu.SemaphoreType.REGULAR,
            dma((5,)),
            dma((4, nz)),
            dma((4, nz)),
            dma((3, 4, nz)),
            dma((4, nz)),
            dma((3, 3)),
            dma((3,)),
            dma((2,)),
            dma,
            dma((4,)),
            dma((7,)),
            dma((7,)),
            dma((2,)),
            dma,
        ],
        compiler_params=pltpu.CompilerParams(
            collective_id=0, has_side_effects=True, vmem_limit_bytes=62 * 1024 * 1024
        ),
    )(
        timesteps,
        latents.reshape(rows, width),
        mod_table,
        *split,
        k_gain.reshape(1, -1),
        q_gain.reshape(1, -1),
    )
    return out.reshape(1, 1, rows, cols)


def solution(mesh):
    sizes = (mesh.shape["rep"], mesh.shape["sp"] // 2, mesh.shape["tp"])
    return jax.shard_map(
        functools.partial(local, sizes),
        mesh=mesh,
        in_specs=(
            P("rep", None, "sp", None),
            P("rep"),
            P(),
            P("rep", "tp"),
            P("rep", "tp"),
            P("rep", "tp"),
            P(),
            P(),
        ),
        out_specs=P("rep", None, "sp", "tp"),
        check_vma=False,
    )
```

```python
import functools

import jax
import jax.numpy as jnp
from jax import lax
from jax.experimental import pallas as pl
from jax.experimental.pallas import tpu as pltpu
from jax.sharding import PartitionSpec as P

HEAD_DIM = 128
OFFSETS = (0, 1, 2, 3)
PAIRS = (False, False, True, True)
LAG_X = 1
LAG_F = (2, 2, 1, 1)
MESH = pl.DeviceIdType.MESH


def dot(a, b, dims=((1,), (0,)), precision=None):
    return lax.dot_general(a, b, (dims, ((), ())), precision=precision, preferred_element_type=jnp.float32)


def kernel(
    sizes,
    steps_ref, latents_hbm, table_hbm, wk_hbm, wq_hbm, wv_hbm, kgain_ref, qgain_ref,
    out_ref,
    wbuf, latents, table, modulation, normed, acc, kvbuf, qbuf, probs, sums, scales, knbuf, answered,
    local_sem, zrecv, zfar, xrecv, srecv, kvrecv, kvsib, sumrecv, scalerecv, zsend, xsend, ssend, sumsend, scalesend,
):
    nz, nx, nt = sizes
    r, s, tp = lax.axis_index("rep"), lax.axis_index("sp"), lax.axis_index("tp")
    x, c = s // 2, s % 2
    step = 1 - 2 * c
    fore, back = (x + step + nx) % nx, (x - step + nx) % nx
    base = c * nx
    mine, of_back, of_fore, of_far = base + x, base + back, base + fore, base + (x + 2) % nx
    to_fore, to_back, to_core = {"sp": fore * 2 + c}, {"sp": back * 2 + c}, {"sp": s + 1 - 2 * c}
    up, down = {"rep": r + 1}, {"rep": r - 1}
    whbm = (wk_hbm, wq_hbm, wv_hbm)
    rows, width = latents.shape
    cols = kvbuf.shape[3]
    heads = cols // HEAD_DIM

    split = cols - HEAD_DIM
    streams = ((0, 0, cols), (1, 0, cols), (2, 0, split), (2, split, cols))
    count = len(streams)

    def weight(m, src, piece):
        which, first, end = streams[m]
        return wbuf.at[which, src, piece, :, pl.ds(first, end - first)]

    shared = ((0, 0, cols), (1, 0, split), (1, split, cols))

    def kv_part(j, piece):
        which, first, end = shared[j]
        return kvbuf.at[which, piece, :, pl.ds(first, end - first)]

    def send(src, dst, send_sem, recv_sem, where):
        pltpu.make_async_remote_copy(src, dst, send_sem, recv_sem, device_id=where, device_id_type=MESH).start()

    def arrived(ref, recv_sem):
        pltpu.make_async_remote_copy(ref, ref, xsend.at[0], recv_sem, device_id=to_fore, device_id_type=MESH).wait_recv()

    def sent(ref, send_sem):
        pltpu.make_async_remote_copy(ref, ref, send_sem, sumrecv.at[0], device_id=to_fore, device_id_type=MESH).wait_send()

    loads = [pltpu.make_async_copy(latents_hbm, latents, local_sem.at[0]),
             pltpu.make_async_copy(table_hbm, table, local_sem.at[1])]
    loads += [pltpu.make_async_copy(whbm[m], wbuf.at[m, r], local_sem.at[2 + m]) for m in range(3)]
    for load in loads:
        load.start()

    barrier = pltpu.get_barrier_semaphore()

    def greet(where):
        pl.semaphore_signal(barrier, inc=1, device_id=where, device_id_type=MESH)

    ny = nt // 2
    lower = tp < ny

    def far_peers(action):
        for i in range(ny):
            action({"tp": (tp + ny) % nt // ny * ny + i})

    for where in (to_fore, to_back, to_core):
        greet(where)
    pl.when(r < nz - 1)(lambda: greet(up))
    pl.when(r > 0)(lambda: greet(down))
    for i in range(1, ny):
        greet({"tp": (tp // ny) * ny + (tp + i) % ny})
    pl.when(lower)(lambda: far_peers(greet))
    at_end = jnp.logical_or(r == 0, r == nz - 1)

    def wait_greetings(near):
        pl.when(lower)(lambda: pl.semaphore_wait(barrier, near))
        pl.when(jnp.logical_not(lower))(lambda: pl.semaphore_wait(barrier, near + ny))

    pl.when(at_end)(lambda: wait_greetings(3 + ny))
    pl.when(jnp.logical_not(at_end))(lambda: wait_greetings(4 + ny))

    def answer(where):
        pl.semaphore_signal(answered, inc=1, device_id=where, device_id_type=MESH)

    pl.when(jnp.logical_not(lower))(lambda: far_peers(answer))

    def both_ways(action):
        pl.when(r < nz - 1)(lambda: action(up, 0))
        pl.when(r > 0)(lambda: action(down, 1))

    def send_own(m):
        def one(where, way):
            send(weight(m, r, mine), weight(m, r, mine), zsend.at[m], zrecv.at[m, r], where)
            if PAIRS[m]:
                send(weight(m, r, of_far), weight(m, r, of_far), zsend.at[m], zfar.at[m, r], where)
        both_ways(one)

    def over_sources(k, least, action):
        pl.when(jnp.logical_and(k >= least, r - k >= 0))(lambda: action(r - k, 0))
        pl.when(jnp.logical_and(k >= least, r + k <= nz - 1))(lambda: action(r + k, 1))

    def z_event(k, m):
        def one(src, way):
            def pass_on(place, sems):
                piece = weight(m, src, place)
                arrived(piece, sems.at[m, src])
                if way == 0:
                    pl.when(r < nz - 1)(lambda: send(piece, piece, zsend.at[m], sems.at[m, src], up))
                else:
                    pl.when(r > 0)(lambda: send(piece, piece, zsend.at[m], sems.at[m, src], down))

            pass_on(mine, zrecv)
            piece = weight(m, src, mine)
            send(piece, piece, xsend.at[m], xrecv.at[0, m, src], to_fore)
            send(piece, piece, xsend.at[m], xrecv.at[1, m, src], to_back)
            if PAIRS[m]:
                pass_on(of_far, zfar)
        over_sources(k, 1, one)

    upper = r // (nz // 2)
    edge = r + upper * (nz - 1 - 2 * r)

    def nth_source(n, action):
        @pl.when(jnp.logical_and(n >= 1, n <= nz - 1))
        def _():
            both = n <= 2 * edge
            sign = jnp.where(both, 2 * ((n - 1) % 2) - 1, 1 - 2 * upper)
            action(r + sign * jnp.where(both, (n + 1) // 2, n - edge))

    def x_event(n, m):
        if PAIRS[m]:
            return

        def one(src):
            piece = weight(m, src, of_back)
            arrived(piece, xrecv.at[0, m, src])
            send(piece, piece, xsend.at[m], xrecv.at[2, m, src], to_fore)
        nth_source(n, one)

    def to_sibling(m, src):
        block = weight(m, src, pl.ds(base, nx))
        send(block, block, ssend.at[m], srecv.at[m, src], to_core)

    def f_event(n, m):
        def one(src):
            arrived(weight(m, src, of_fore), xrecv.at[1, m, src])
            if PAIRS[m]:
                arrived(weight(m, src, of_back), xrecv.at[0, m, src])
            else:
                arrived(weight(m, src, of_far), xrecv.at[2, m, src])
            to_sibling(m, src)
        nth_source(n, one)

    norm_count = 4
    norm_rows = rows // norm_count

    def add_source(m, src):
        depth = width // nz
        at = pl.ds(pl.multiple_of(src * depth, HEAD_DIM), depth)
        which, first, end = streams[m]
        acc[which, :, first:end] += dot(normed[:, at], wbuf[which, src, :, :, first:end].reshape(depth, end - first))

    def use(m, src):
        arrived(weight(m, src, pl.ds(base, nx)), srecv.at[m, src])
        add_source(m, src)

    def use_nth(n, m):
        nth_source(n, lambda src: use(m, src))

    def g_event(n, m):
        ready = jnp.logical_and(n + OFFSETS[m] + LAG_F[m] + 1 > norm_count, n < nz - 1 if m < 2 else n < nz)
        pl.when(ready)(lambda: use_nth(n, m))

    def slot(t):
        for m in range(count):
            z_event(t - OFFSETS[m], m)
        for m in range(count):
            x_event(t - OFFSETS[m] - LAG_X, m)
        for m in range(count):
            f_event(t - OFFSETS[m] - LAG_F[m], m)
        for m in range(count):
            g_event(t - OFFSETS[m] - LAG_F[m] - 1, m)

    def slots(first, end, extra=None):
        @pl.loop(first, end)
        def _(t):
            slot(t)
            if extra is not None:
                extra(t - first)


    def norm_block(i):
        at = pl.ds(pl.multiple_of(i * norm_rows, norm_rows), norm_rows)
        values = latents[at, :].astype(jnp.float32)
        center = values - jnp.mean(values, axis=-1, keepdims=True)
        spread = jnp.mean(center * center, axis=-1, keepdims=True)
        scaled = center * lax.rsqrt(spread + 1e-06) * modulation[1:2, :] + modulation[0:1, :]
        normed[at, :] = scaled.astype(jnp.bfloat16)

    def send_sums(i, values):
        wide = values.astype(jnp.float32)
        square = dot(jnp.ones((8, cols), jnp.float32), wide * wide, ((1,), (1,)), lax.Precision.HIGHEST)
        sums[i, tp] = jnp.zeros(sums.shape[2:], jnp.float32)
        sums[i, tp, :, 0:rows] = square[0:1]
        for j in range(1, nt):
            send(sums.at[i, tp], sums.at[i, tp], sumsend.at[i], sumrecv.at[i], {"tp": (tp + j) % nt})

    def inverse_rms(i):
        arrived(sums.at[i, pl.ds(0, nt - 1)], sumrecv.at[i])
        total = sums[i, 0]
        for j in range(1, nt):
            total = total + sums[i, j]
        return lax.rsqrt(total * (1.0 / (nt * cols)) + 1e-06)

    def gain_of(gain_ref):
        return gain_ref[:, pl.ds(pl.multiple_of(tp * cols, HEAD_DIM), cols)]

    def share_key_scale():
        scales[mine] = inverse_rms(0)
        for j in range(1, 2 * nx):
            send(scales.at[mine], scales.at[mine], scalesend, scalerecv, {"sp": (s + j) % (2 * nx)})

    def normalise(values, scale, gain_ref):
        column = jnp.concatenate(
            [jnp.transpose(jnp.broadcast_to(scale[:, j : j + 128], (128, 128))) for j in range(0, scale.shape[1], 128)],
            axis=0,
        )[0:rows]
        wide = values.astype(jnp.float32) * gain_of(gain_ref)
        parts = [wide[:, h * 128 : (h + 1) * 128] * column for h in range(heads)]
        return jnp.concatenate(parts, axis=1).astype(jnp.bfloat16)

    def normalise_keys():
        arrived(scales.at[pl.ds(0, 2 * nx - 1)], scalerecv)

        @pl.loop(0, 2 * nx)
        def _(j):
            knbuf[j] = normalise(kvbuf[0, j], scales[j], kgain_ref)

    def kv_send(j):
        block = kv_part(j, mine)
        send(block, block, xsend.at[count + j], kvrecv.at[0, j], to_fore)
        send(block, block, xsend.at[count + j], kvrecv.at[1, j], to_back)
        if j > 0:
            send(block, block, xsend.at[count + j], kvrecv.at[2, j], {"sp": (x + 2) % nx * 2 + c})
        send(block, block, ssend.at[count + j], kvsib.at[j], to_core)

    def kv_pass(j):
        block = kv_part(j, of_back)
        arrived(block, kvrecv.at[0, j])
        if j == 0:
            send(block, block, xsend.at[count + j], kvrecv.at[2, j], to_fore)
        send(block, block, ssend.at[count + j], kvsib.at[j], to_core)

    def kv_far(j):
        for kind, piece in ((1, of_fore), (2, of_far)):
            block = kv_part(j, piece)
            arrived(block, kvrecv.at[kind, j])
            send(block, block, ssend.at[count + j], kvsib.at[j], to_core)

    for load in loads[2:]:
        load.wait()
    send_own(0)
    send_own(1)
    acc[...] = jnp.zeros_like(acc)
    loads[1].wait()
    modulation[...] = table[steps_ref[0]]
    modulation[1:2, :] = modulation[1:2, :] + 1.0
    loads[0].wait()

    def early(i):
        norm_block(i)
        for m in range(2, count):
            pl.when(i == OFFSETS[m] - 1)(functools.partial(send_own, m))

    done = 1 + norm_count
    slots(1, done, early)
    for m in range(count):
        add_source(m, r)
        for n in range(1, norm_count - OFFSETS[m] - LAG_F[m]):
            use_nth(n, m)
    ends = [nz + at + lag for at, lag in zip(OFFSETS, LAG_F)]
    slots(done, ends[0])
    use_nth(nz - 1, 0)
    kvbuf[0, mine] = acc[0].astype(jnp.bfloat16)
    kv_send(0)
    pl.when(lower)(lambda: pl.semaphore_wait(answered, ny))
    send_sums(0, kvbuf[0, mine])
    slots(ends[0], ends[1])
    use_nth(nz - 1, 1)
    qbuf[...] = acc[1].astype(jnp.bfloat16)
    send_sums(1, qbuf[...])
    kv_pass(0)
    slots(ends[1], ends[2] + 1)
    kvbuf[1, mine, :, 0:split] = acc[2, :, 0:split].astype(jnp.bfloat16)
    kv_send(1)
    kv_far(0)
    share_key_scale()
    slots(ends[2] + 1, ends[3] + 1)
    kvbuf[1, mine, :, split:cols] = acc[2, :, split:cols].astype(jnp.bfloat16)
    kv_send(2)
    arrived(kv_part(0, pl.ds(0, nx)), kvsib.at[0])
    normalise_keys()
    qbuf[...] = normalise(qbuf[...], inverse_rms(1), qgain_ref)

    inverse_root = 1.0 / HEAD_DIM**0.5
    keys_all = 2 * nx * rows
    totals = []
    for h in range(heads):
        at = slice(h * HEAD_DIM, (h + 1) * HEAD_DIM)
        scores = dot(qbuf[:, at], knbuf[:, :, at].reshape(keys_all, HEAD_DIM), ((1,), (1,))) * inverse_root
        weights = jnp.exp(scores - jnp.max(scores, axis=-1, keepdims=True))
        totals.append(jnp.sum(weights, axis=-1, keepdims=True))
        probs[h] = weights.astype(jnp.bfloat16)
        if h < 2:
            kv_pass(1 + h)
            kv_far(1 + h)
    arrived(kv_part(1, pl.ds(0, nx)), kvsib.at[1])
    for h in range(heads):
        at = slice(h * HEAD_DIM, (h + 1) * HEAD_DIM)
        if h == heads - 1:
            arrived(kv_part(2, pl.ds(0, nx)), kvsib.at[2])
        context = dot(probs[h], kvbuf[1, :, :, at].reshape(keys_all, HEAD_DIM)) / totals[h]
        out_ref[:, at] = context.astype(jnp.bfloat16)


    def pieces(m, copies):
        outer = max(a for a in range(1, nz + 1) if copies % a == 0 and copies // a <= 2 * nx)
        return weight(m, pl.ds(0, outer), pl.ds(0, copies // outer))

    def wait_sends(copies):
        for m in range(count):
            sent(pieces(m, copies * (2 if PAIRS[m] else 1)), zsend.at[m])

    pl.when(edge > 0)(lambda: wait_sends(nz + 1))
    pl.when(edge == 0)(lambda: wait_sends(1))
    for m in range(count):
        sent(pieces(m, (nz - 1) * (2 if PAIRS[m] else 3)), xsend.at[m])
    for m in range(count):
        sent(weight(m, pl.ds(0, nz - 1), pl.ds(0, nx)), ssend.at[m])
    for j in range(3):
        sent(kv_part(j, pl.ds(0, 3)), xsend.at[count + j])
        sent(kv_part(j, pl.ds(0, nx)), ssend.at[count + j])
    for j in range(2):
        sent(sums.at[j, pl.ds(0, nt - 1)], sumsend.at[j])
    sent(scales.at[pl.ds(0, 2 * nx - 1)], scalesend)


def local(sizes, latents, timesteps, mod_table, w_query, w_key, w_value, q_gain, k_gain):
    nz, nx, nt = sizes
    rows, width = latents.shape[2:]
    cols = w_query.shape[1]
    part = w_query.shape[0] // (2 * nx)
    hbm, vmem = pl.BlockSpec(memory_space=pl.ANY), pl.BlockSpec(memory_space=pltpu.VMEM)
    split = [w.reshape(2 * nx, part, cols) for w in (w_key, w_query, w_value)]
    dma = pltpu.SemaphoreType.DMA
    out = pl.pallas_call(
        functools.partial(kernel, sizes),
        out_shape=jax.ShapeDtypeStruct((rows, cols), jnp.bfloat16),
        in_specs=[pl.BlockSpec(memory_space=pltpu.SMEM), hbm, hbm, hbm, hbm, hbm, vmem, vmem],
        out_specs=vmem,
        scratch_shapes=[
            pltpu.VMEM((3, nz, 2 * nx, part, cols), jnp.bfloat16),
            pltpu.VMEM((rows, width), jnp.bfloat16),
            pltpu.VMEM(mod_table.shape, jnp.float32),
            pltpu.VMEM((2, width), jnp.float32),
            pltpu.VMEM((rows, width), jnp.bfloat16),
            pltpu.VMEM((3, rows, cols), jnp.float32),
            pltpu.VMEM((2, 2 * nx, rows, cols), jnp.bfloat16),
            pltpu.VMEM((rows, cols), jnp.bfloat16),
            pltpu.VMEM((cols // HEAD_DIM, rows, 2 * nx * rows), jnp.bfloat16),
            pltpu.VMEM((2, nt, 1, (rows + 127) // 128 * 128), jnp.float32),
            pltpu.VMEM((2 * nx, 1, (rows + 127) // 128 * 128), jnp.float32),
            pltpu.VMEM((2 * nx, rows, cols), jnp.bfloat16),
            pltpu.SemaphoreType.REGULAR,
            dma((5,)),
            dma((4, nz)),
            dma((4, nz)),
            dma((3, 4, nz)),
            dma((4, nz)),
            dma((3, 3)),
            dma((3,)),
            dma((2,)),
            dma,
            dma((4,)),
            dma((7,)),
            dma((7,)),
            dma((2,)),
            dma,
        ],
        compiler_params=pltpu.CompilerParams(
            collective_id=0, has_side_effects=True, vmem_limit_bytes=62 * 1024 * 1024
        ),
    )(
        timesteps,
        latents.reshape(rows, width),
        mod_table,
        *split,
        k_gain.reshape(1, -1),
        q_gain.reshape(1, -1),
    )
    return out.reshape(1, 1, rows, cols)


def solution(mesh):
    sizes = (mesh.shape["rep"], mesh.shape["sp"] // 2, mesh.shape["tp"])
    return jax.shard_map(
        functools.partial(local, sizes),
        mesh=mesh,
        in_specs=(
            P("rep", None, "sp", None),
            P("rep"),
            P(),
            P("rep", "tp"),
            P("rep", "tp"),
            P("rep", "tp"),
            P(),
            P(),
        ),
        out_specs=P("rep", None, "sp", "tp"),
        check_vma=False,
    )
```

```python
import functools

import jax
import jax.numpy as jnp
from jax import lax
from jax.experimental import pallas as pl
from jax.experimental.pallas import tpu as pltpu
from jax.sharding import PartitionSpec as P

HEAD_DIM = 128
OFFSETS = (0, 1, 2, 3)
PAIRS = (False, False, True, True)
LAG_X = 1
LAG_F = (2, 2, 1, 1)
MESH = pl.DeviceIdType.MESH


def dot(a, b, dims=((1,), (0,)), precision=None):
    return lax.dot_general(a, b, (dims, ((), ())), precision=precision, preferred_element_type=jnp.float32)


def kernel(
    sizes,
    steps_ref, latents_hbm, table_hbm, wk_hbm, wq_hbm, wv_hbm, kgain_ref, qgain_ref,
    out_ref,
    wbuf, latents, table, modulation, normed, acc, kvbuf, qbuf, probs, sums, scales, knbuf, answered,
    local_sem, zrecv, zfar, xrecv, srecv, kvrecv, kvsib, sumrecv, scalerecv, zsend, xsend, ssend, sumsend, scalesend,
):
    nz, nx, nt = sizes
    r, s, tp = lax.axis_index("rep"), lax.axis_index("sp"), lax.axis_index("tp")
    x, c = s // 2, s % 2
    step = 1 - 2 * c
    fore, back = (x + step + nx) % nx, (x - step + nx) % nx
    base = c * nx
    mine, of_back, of_fore, of_far = base + x, base + back, base + fore, base + (x + 2) % nx
    to_fore, to_back, to_core = {"sp": fore * 2 + c}, {"sp": back * 2 + c}, {"sp": s + 1 - 2 * c}
    up, down = {"rep": r + 1}, {"rep": r - 1}
    whbm = (wk_hbm, wq_hbm, wv_hbm)
    rows, width = latents.shape
    cols = kvbuf.shape[3]
    heads = cols // HEAD_DIM

    split = cols - HEAD_DIM
    streams = ((0, 0, cols), (1, 0, cols), (2, 0, split), (2, split, cols))
    count = len(streams)

    def weight(m, src, piece):
        which, first, end = streams[m]
        return wbuf.at[which, src, piece, :, pl.ds(first, end - first)]

    shared = ((0, 0, cols), (1, 0, split), (1, split, cols))

    def kv_part(j, piece):
        which, first, end = shared[j]
        return kvbuf.at[which, piece, :, pl.ds(first, end - first)]

    def send(src, dst, send_sem, recv_sem, where):
        pltpu.make_async_remote_copy(src, dst, send_sem, recv_sem, device_id=where, device_id_type=MESH).start()

    def arrived(ref, recv_sem):
        pltpu.make_async_remote_copy(ref, ref, xsend.at[0], recv_sem, device_id=to_fore, device_id_type=MESH).wait_recv()

    def sent(ref, send_sem):
        pltpu.make_async_remote_copy(ref, ref, send_sem, sumrecv.at[0], device_id=to_fore, device_id_type=MESH).wait_send()

    loads = [pltpu.make_async_copy(latents_hbm, latents, local_sem.at[0]),
             pltpu.make_async_copy(table_hbm, table, local_sem.at[1])]
    loads += [pltpu.make_async_copy(whbm[m], wbuf.at[m, r], local_sem.at[2 + m]) for m in range(3)]
    barrier = pltpu.get_barrier_semaphore()

    def greet(where):
        pl.semaphore_signal(barrier, inc=1, device_id=where, device_id_type=MESH)

    ny = nt // 2
    lower = tp < ny

    def far_peers(action):
        for i in range(ny):
            action({"tp": (tp + ny) % nt // ny * ny + i})

    for where in (to_fore, to_back, to_core):
        greet(where)
    pl.when(r < nz - 1)(lambda: greet(up))
    pl.when(r > 0)(lambda: greet(down))
    for i in range(1, ny):
        greet({"tp": (tp // ny) * ny + (tp + i) % ny})
    pl.when(lower)(lambda: far_peers(greet))
    at_end = jnp.logical_or(r == 0, r == nz - 1)

    def wait_greetings(near):
        pl.when(lower)(lambda: pl.semaphore_wait(barrier, near))
        pl.when(jnp.logical_not(lower))(lambda: pl.semaphore_wait(barrier, near + ny))

    for load in loads:
        load.start()
    pl.when(at_end)(lambda: wait_greetings(3 + ny))
    pl.when(jnp.logical_not(at_end))(lambda: wait_greetings(4 + ny))

    def answer(where):
        pl.semaphore_signal(answered, inc=1, device_id=where, device_id_type=MESH)

    pl.when(jnp.logical_not(lower))(lambda: far_peers(answer))

    def both_ways(action):
        pl.when(r < nz - 1)(lambda: action(up, 0))
        pl.when(r > 0)(lambda: action(down, 1))

    def send_own(m):
        def one(where, way):
            send(weight(m, r, mine), weight(m, r, mine), zsend.at[m], zrecv.at[m, r], where)
            if PAIRS[m]:
                send(weight(m, r, of_far), weight(m, r, of_far), zsend.at[m], zfar.at[m, r], where)
        both_ways(one)

    def over_sources(k, least, action):
        pl.when(jnp.logical_and(k >= least, r - k >= 0))(lambda: action(r - k, 0))
        pl.when(jnp.logical_and(k >= least, r + k <= nz - 1))(lambda: action(r + k, 1))

    def z_event(k, m):
        def one(src, way):
            def pass_on(place, sems):
                piece = weight(m, src, place)
                arrived(piece, sems.at[m, src])
                if way == 0:
                    pl.when(r < nz - 1)(lambda: send(piece, piece, zsend.at[m], sems.at[m, src], up))
                else:
                    pl.when(r > 0)(lambda: send(piece, piece, zsend.at[m], sems.at[m, src], down))

            pass_on(mine, zrecv)
            piece = weight(m, src, mine)
            send(piece, piece, xsend.at[m], xrecv.at[0, m, src], to_fore)
            send(piece, piece, xsend.at[m], xrecv.at[1, m, src], to_back)
            if PAIRS[m]:
                pass_on(of_far, zfar)
        over_sources(k, 1, one)

    upper = r // (nz // 2)
    edge = r + upper * (nz - 1 - 2 * r)

    def nth_source(n, action):
        @pl.when(jnp.logical_and(n >= 1, n <= nz - 1))
        def _():
            both = n <= 2 * edge
            sign = jnp.where(both, 2 * ((n - 1) % 2) - 1, 1 - 2 * upper)
            action(r + sign * jnp.where(both, (n + 1) // 2, n - edge))

    def x_event(n, m):
        if PAIRS[m]:
            return

        def one(src):
            piece = weight(m, src, of_back)
            arrived(piece, xrecv.at[0, m, src])
            send(piece, piece, xsend.at[m], xrecv.at[2, m, src], to_fore)
        nth_source(n, one)

    def to_sibling(m, src):
        block = weight(m, src, pl.ds(base, nx))
        send(block, block, ssend.at[m], srecv.at[m, src], to_core)

    def f_event(n, m):
        def one(src):
            arrived(weight(m, src, of_fore), xrecv.at[1, m, src])
            if PAIRS[m]:
                arrived(weight(m, src, of_back), xrecv.at[0, m, src])
            else:
                arrived(weight(m, src, of_far), xrecv.at[2, m, src])
            to_sibling(m, src)
        nth_source(n, one)

    norm_count = 4
    norm_rows = rows // norm_count

    def add_source(m, src):
        depth = width // nz
        at = pl.ds(pl.multiple_of(src * depth, HEAD_DIM), depth)
        which, first, end = streams[m]
        acc[which, :, first:end] += dot(normed[:, at], wbuf[which, src, :, :, first:end].reshape(depth, end - first))

    def use(m, src):
        arrived(weight(m, src, pl.ds(base, nx)), srecv.at[m, src])
        add_source(m, src)

    def use_nth(n, m):
        nth_source(n, lambda src: use(m, src))

    def g_event(n, m):
        ready = jnp.logical_and(n + OFFSETS[m] + LAG_F[m] + 1 > norm_count, n < nz - 1 if m < 2 else n < nz)
        pl.when(ready)(lambda: use_nth(n, m))

    def slot(t):
        for m in range(count):
            z_event(t - OFFSETS[m], m)
        for m in range(count):
            x_event(t - OFFSETS[m] - LAG_X, m)
        for m in range(count):
            f_event(t - OFFSETS[m] - LAG_F[m], m)
        for m in range(count):
            g_event(t - OFFSETS[m] - LAG_F[m] - 1, m)

    def slots(first, end, extra=None):
        @pl.loop(first, end)
        def _(t):
            slot(t)
            if extra is not None:
                extra(t - first)


    def norm_block(i):
        at = pl.ds(pl.multiple_of(i * norm_rows, norm_rows), norm_rows)
        values = latents[at, :].astype(jnp.float32)
        center = values - jnp.mean(values, axis=-1, keepdims=True)
        spread = jnp.mean(center * center, axis=-1, keepdims=True)
        scaled = center * lax.rsqrt(spread + 1e-06) * modulation[1:2, :] + modulation[0:1, :]
        normed[at, :] = scaled.astype(jnp.bfloat16)

    def send_sums(i, values):
        wide = values.astype(jnp.float32)
        square = dot(jnp.ones((8, cols), jnp.float32), wide * wide, ((1,), (1,)), lax.Precision.HIGHEST)
        sums[i, tp] = jnp.zeros(sums.shape[2:], jnp.float32)
        sums[i, tp, :, 0:rows] = square[0:1]
        for j in range(1, nt):
            send(sums.at[i, tp], sums.at[i, tp], sumsend.at[i], sumrecv.at[i], {"tp": (tp + j) % nt})

    def inverse_rms(i):
        arrived(sums.at[i, pl.ds(0, nt - 1)], sumrecv.at[i])
        total = sums[i, 0]
        for j in range(1, nt):
            total = total + sums[i, j]
        return lax.rsqrt(total * (1.0 / (nt * cols)) + 1e-06)

    def gain_of(gain_ref):
        return gain_ref[:, pl.ds(pl.multiple_of(tp * cols, HEAD_DIM), cols)]

    def share_key_scale():
        scales[mine] = inverse_rms(0)
        for j in range(1, 2 * nx):
            send(scales.at[mine], scales.at[mine], scalesend, scalerecv, {"sp": (s + j) % (2 * nx)})

    def normalise(values, scale, gain_ref):
        column = jnp.concatenate(
            [jnp.transpose(jnp.broadcast_to(scale[:, j : j + 128], (128, 128))) for j in range(0, scale.shape[1], 128)],
            axis=0,
        )[0:rows]
        wide = values.astype(jnp.float32) * gain_of(gain_ref)
        parts = [wide[:, h * 128 : (h + 1) * 128] * column for h in range(heads)]
        return jnp.concatenate(parts, axis=1).astype(jnp.bfloat16)

    def normalise_keys():
        arrived(scales.at[pl.ds(0, 2 * nx - 1)], scalerecv)

        @pl.loop(0, 2 * nx)
        def _(j):
            knbuf[j] = normalise(kvbuf[0, j], scales[j], kgain_ref)

    def kv_send(j):
        block = kv_part(j, mine)
        send(block, block, xsend.at[count + j], kvrecv.at[0, j], to_fore)
        send(block, block, xsend.at[count + j], kvrecv.at[1, j], to_back)
        if j > 0:
            send(block, block, xsend.at[count + j], kvrecv.at[2, j], {"sp": (x + 2) % nx * 2 + c})
        send(block, block, ssend.at[count + j], kvsib.at[j], to_core)

    def kv_pass(j):
        block = kv_part(j, of_back)
        arrived(block, kvrecv.at[0, j])
        if j == 0:
            send(block, block, xsend.at[count + j], kvrecv.at[2, j], to_fore)
        send(block, block, ssend.at[count + j], kvsib.at[j], to_core)

    def kv_far(j):
        for kind, piece in ((1, of_fore), (2, of_far)):
            block = kv_part(j, piece)
            arrived(block, kvrecv.at[kind, j])
            send(block, block, ssend.at[count + j], kvsib.at[j], to_core)

    for load in loads[2:]:
        load.wait()
    send_own(0)
    send_own(1)
    acc[...] = jnp.zeros_like(acc)
    loads[1].wait()
    modulation[...] = table[steps_ref[0]]
    modulation[1:2, :] = modulation[1:2, :] + 1.0
    loads[0].wait()

    def early(i):
        norm_block(i)
        for m in range(2, count):
            pl.when(i == OFFSETS[m] - 1)(functools.partial(send_own, m))

    done = 1 + norm_count
    slots(1, done, early)
    for m in range(count):
        add_source(m, r)
        for n in range(1, norm_count - OFFSETS[m] - LAG_F[m]):
            use_nth(n, m)
    ends = [nz + at + lag for at, lag in zip(OFFSETS, LAG_F)]
    slots(done, ends[0])
    use_nth(nz - 1, 0)
    kvbuf[0, mine] = acc[0].astype(jnp.bfloat16)
    pl.when(lower)(lambda: pl.semaphore_wait(answered, ny))
    send_sums(0, kvbuf[0, mine])
    kv_send(0)
    slots(ends[0], ends[1])
    use_nth(nz - 1, 1)
    qbuf[...] = acc[1].astype(jnp.bfloat16)
    send_sums(1, qbuf[...])
    kv_pass(0)
    slots(ends[1], ends[2] + 1)
    kvbuf[1, mine, :, 0:split] = acc[2, :, 0:split].astype(jnp.bfloat16)
    kv_send(1)
    kv_far(0)
    share_key_scale()
    slots(ends[2] + 1, ends[3] + 1)
    kvbuf[1, mine, :, split:cols] = acc[2, :, split:cols].astype(jnp.bfloat16)
    kv_send(2)
    arrived(kv_part(0, pl.ds(0, nx)), kvsib.at[0])
    normalise_keys()
    qbuf[...] = normalise(qbuf[...], inverse_rms(1), qgain_ref)

    inverse_root = 1.0 / HEAD_DIM**0.5
    keys_all = 2 * nx * rows
    totals = []
    for h in range(heads):
        at = slice(h * HEAD_DIM, (h + 1) * HEAD_DIM)
        scores = dot(qbuf[:, at], knbuf[:, :, at].reshape(keys_all, HEAD_DIM), ((1,), (1,))) * inverse_root
        weights = jnp.exp(scores - jnp.max(scores, axis=-1, keepdims=True))
        totals.append(jnp.sum(weights, axis=-1, keepdims=True))
        probs[h] = weights.astype(jnp.bfloat16)
        if h < 2:
            kv_pass(1 + h)
            kv_far(1 + h)
    arrived(kv_part(1, pl.ds(0, nx)), kvsib.at[1])
    for h in range(heads):
        at = slice(h * HEAD_DIM, (h + 1) * HEAD_DIM)
        if h == heads - 1:
            arrived(kv_part(2, pl.ds(0, nx)), kvsib.at[2])
        context = dot(probs[h], kvbuf[1, :, :, at].reshape(keys_all, HEAD_DIM)) / totals[h]
        out_ref[:, at] = context.astype(jnp.bfloat16)


    def pieces(m, copies):
        outer = max(a for a in range(1, nz + 1) if copies % a == 0 and copies // a <= 2 * nx)
        return weight(m, pl.ds(0, outer), pl.ds(0, copies // outer))

    def wait_sends(copies):
        for m in range(count):
            sent(pieces(m, copies * (2 if PAIRS[m] else 1)), zsend.at[m])

    pl.when(edge > 0)(lambda: wait_sends(nz + 1))
    pl.when(edge == 0)(lambda: wait_sends(1))
    for m in range(count):
        sent(pieces(m, (nz - 1) * (2 if PAIRS[m] else 3)), xsend.at[m])
    for m in range(count):
        sent(weight(m, pl.ds(0, nz - 1), pl.ds(0, nx)), ssend.at[m])
    for j in range(3):
        sent(kv_part(j, pl.ds(0, 3)), xsend.at[count + j])
        sent(kv_part(j, pl.ds(0, nx)), ssend.at[count + j])
    for j in range(2):
        sent(sums.at[j, pl.ds(0, nt - 1)], sumsend.at[j])
    sent(scales.at[pl.ds(0, 2 * nx - 1)], scalesend)


def local(sizes, latents, timesteps, mod_table, w_query, w_key, w_value, q_gain, k_gain):
    nz, nx, nt = sizes
    rows, width = latents.shape[2:]
    cols = w_query.shape[1]
    part = w_query.shape[0] // (2 * nx)
    hbm, vmem = pl.BlockSpec(memory_space=pl.ANY), pl.BlockSpec(memory_space=pltpu.VMEM)
    split = [w.reshape(2 * nx, part, cols) for w in (w_key, w_query, w_value)]
    dma = pltpu.SemaphoreType.DMA
    out = pl.pallas_call(
        functools.partial(kernel, sizes),
        out_shape=jax.ShapeDtypeStruct((rows, cols), jnp.bfloat16),
        in_specs=[pl.BlockSpec(memory_space=pltpu.SMEM), hbm, hbm, hbm, hbm, hbm, vmem, vmem],
        out_specs=vmem,
        scratch_shapes=[
            pltpu.VMEM((3, nz, 2 * nx, part, cols), jnp.bfloat16),
            pltpu.VMEM((rows, width), jnp.bfloat16),
            pltpu.VMEM(mod_table.shape, jnp.float32),
            pltpu.VMEM((2, width), jnp.float32),
            pltpu.VMEM((rows, width), jnp.bfloat16),
            pltpu.VMEM((3, rows, cols), jnp.float32),
            pltpu.VMEM((2, 2 * nx, rows, cols), jnp.bfloat16),
            pltpu.VMEM((rows, cols), jnp.bfloat16),
            pltpu.VMEM((cols // HEAD_DIM, rows, 2 * nx * rows), jnp.bfloat16),
            pltpu.VMEM((2, nt, 1, (rows + 127) // 128 * 128), jnp.float32),
            pltpu.VMEM((2 * nx, 1, (rows + 127) // 128 * 128), jnp.float32),
            pltpu.VMEM((2 * nx, rows, cols), jnp.bfloat16),
            pltpu.SemaphoreType.REGULAR,
            dma((5,)),
            dma((4, nz)),
            dma((4, nz)),
            dma((3, 4, nz)),
            dma((4, nz)),
            dma((3, 3)),
            dma((3,)),
            dma((2,)),
            dma,
            dma((4,)),
            dma((7,)),
            dma((7,)),
            dma((2,)),
            dma,
        ],
        compiler_params=pltpu.CompilerParams(
            collective_id=0, has_side_effects=True, vmem_limit_bytes=62 * 1024 * 1024
        ),
    )(
        timesteps,
        latents.reshape(rows, width),
        mod_table,
        *split,
        k_gain.reshape(1, -1),
        q_gain.reshape(1, -1),
    )
    return out.reshape(1, 1, rows, cols)


def solution(mesh):
    sizes = (mesh.shape["rep"], mesh.shape["sp"] // 2, mesh.shape["tp"])
    return jax.shard_map(
        functools.partial(local, sizes),
        mesh=mesh,
        in_specs=(
            P("rep", None, "sp", None),
            P("rep"),
            P(),
            P("rep", "tp"),
            P("rep", "tp"),
            P("rep", "tp"),
            P(),
            P(),
        ),
        out_specs=P("rep", None, "sp", "tp"),
        check_vma=False,
    )
```
